512 devices in a mesh: role: 4 (over x), cls: 128 (over y, z, core).
Axes of the slice: x: 4, y: 8, z: 8, core: 2. Of those that a mesh axis runs over, the one named last changes fastest.
Arguments:
- features: bfloat16 [1024, 512], P('cls', 'role'), may hold values from -160 to 160, as said below
- centres: bfloat16 [1572864, 512], P(('role', 'cls')), may hold values from -0.25 to 0.25
- samples: int32 [512, 1024], P(('role', 'cls')), may hold values from 0 to 3071, as said below
- counts: int32 [512], P(('role', 'cls')), may hold values from 64 to 1024, as said below
- label_row: int32 [1024], replicated, may hold values from 0 to 3071, as said below
- owner: int32 [1024], replicated, may hold values from 0 to 511, as said below
Outputs:
- feature_grad: float32 [1024, 512], P('cls', 'role')
- centre_grad: bfloat16 [512, 1024, 512], P(('role', 'cls'))
- loss: float32 [1024], P('cls')
The draws below stay inside these ranges and needn't reach their ends.
Inputs may be any that keep to these rules, and one draw needn't show every extreme that they name: `features`: scaled values with spread per image and per feature. `samples`: entries of one shard are distinct; only the first counts[q] entries of shard q are used. `counts`: each count is 1024 divided by 1, 2, 4, 8 or 16; some shard has exactly 1024. label_row[i] stands among the first counts[owner[i]] entries of samples[owner[i]]. `owner`: index of the owning shard along role+cls; shards with more used slots own more images.
All inputs are finite; a program needn't handle non-finite values.
Results may differ from the reference program's by a relative error of at most 0.0061.
Values may be sent and summed in bfloat16 or wider, within the bound.
A program may use at most 64 MiB of HBM per device.

```python
import math
import jax
import jax.numpy as jnp
from jax import lax

D = 512
CEN_DEV = 3072
SAMP = 1024
SHARDS = 512
CENTRES = 1572864
IMAGES = 1024


def sampling(key):
    shard_keys = jax.random.split(jax.random.fold_in(key, 101), SHARDS)

    def one_list(shard_key):
        return jax.random.permutation(shard_key, CEN_DEV)[:SAMP]
    id_lists = jax.vmap(one_list)(shard_keys).astype(jnp.int32)
    halving = jax.random.randint(jax.random.fold_in(key, 102), (SHARDS,), 0, 5).astype(jnp.int32)
    fullest = jax.random.randint(jax.random.fold_in(key, 103), (), 0, SHARDS).astype(jnp.int32)
    halving = jnp.where(jnp.arange(SHARDS, dtype=jnp.int32) == fullest, 0, halving)
    filled = jnp.right_shift(jnp.full((SHARDS,), SAMP, jnp.int32), halving)
    run_ends = jnp.cumsum(filled).astype(jnp.int32)
    run_starts = run_ends - filled
    drawn = jax.random.randint(jax.random.fold_in(key, 104), (IMAGES,), 0, run_ends[-1]).astype(jnp.int32)
    holder = jnp.sum((run_ends[None, :] <= drawn[:, None]).astype(jnp.int32), 1)
    offset = drawn - run_starts[holder]
    chosen = id_lists[holder, offset]
    return (id_lists, filled, chosen, holder)


def draw_samples(key, part):
    return sampling(key)[0]


def draw_counts(key, part):
    return sampling(key)[1]


def draw_label_row(key, part):
    return sampling(key)[2]


def draw_owner(key, part):
    return sampling(key)[3]


def draw_features(key, part):
    key = jax.random.fold_in(key, 7)
    row_pos = jnp.arange(IMAGES, dtype=jnp.float32) / IMAGES
    col_pos = jnp.arange(D, dtype=jnp.float32) / D
    row_scale = 3.0 ** (row_pos - 0.5) * 10.0 ** (jax.random.uniform(jax.random.fold_in(key, 1), (IMAGES,)) - 0.5)
    col_scale = 3.0 ** (col_pos - 0.5) * 10.0 ** (jax.random.uniform(jax.random.fold_in(key, 2), (D,)) - 0.5)
    col_shift = jax.random.uniform(jax.random.fold_in(key, 3), (D,), minval=-1.0, maxval=1.0)
    base = jnp.clip(jax.random.normal(jax.random.fold_in(key, 4), (IMAGES, D)), -4.0, 4.0)
    values = col_scale[None, :] * (col_shift[None, :] + base * row_scale[:, None])
    return values.astype(jnp.bfloat16)


def levels(rng, shape, cuts, low, top_value):
    loudness = 1.0
    for position, parts in cuts:
        heights = jax.random.uniform(jax.random.fold_in(jax.random.fold_in(rng, 6), position), (parts,), jnp.float32, low / len(cuts), top_value / len(cuts))
        loudness = loudness * jnp.repeat(jnp.exp(heights), shape[position] // parts).reshape((-1,) + (1,) * (len(shape) - 1 - position))
    return loudness


def scatter_about(key, extent, width, limit, cuts=(), held_as=jnp.bfloat16):
    values = jax.random.normal(key, extent, jnp.float32) * width
    if len(cuts) > 0:
        values = levels(key, extent, cuts, -0.22, 0.18) * values
    return jnp.clip(values, min=-limit, max=limit).astype(held_as)


def setup_inputs(seed: int = 0) -> dict:
    streams_of = jax.random.split(jax.random.key(seed), 7)
    features = draw_features(jax.random.fold_in(streams_of[6], 71), 0)
    centres = scatter_about(streams_of[1], (CENTRES, D), D ** -0.5, 0.25, ((0, 512),))
    samples = draw_samples(jax.random.fold_in(streams_of[6], 71), 0)
    counts = draw_counts(jax.random.fold_in(streams_of[6], 71), 0)
    label_row = draw_label_row(jax.random.fold_in(streams_of[6], 71), 0)
    owner = draw_owner(jax.random.fold_in(streams_of[6], 71), 0)
    return dict(features=features, centres=centres, samples=samples, counts=counts, label_row=label_row, owner=owner)


logit_scale = 64.0
margin_cos = math.cos(0.5)
margin_sin = math.sin(0.5)
epsilon = 1e-05

def shard_terms(gathered, block, row_ids, live_count, shard_id, label_row, owner):
    picked = jnp.take(block, row_ids, axis=0).astype(jnp.float32)
    w_inv = lax.rsqrt(lax.optimization_barrier(jnp.sum(picked * picked, 1)) + epsilon)
    w_unit = picked * w_inv[:, None]
    w_round = w_unit.astype(jnp.bfloat16)
    cosine = jnp.dot(gathered.astype(jnp.float32), w_round.astype(jnp.float32).T)
    slot_ids = jnp.arange(row_ids.shape[0], dtype=jnp.int32)
    usable = slot_ids < live_count
    positive = (owner[:, None] == shard_id) & (label_row[:, None] == row_ids[None, :]) & usable[None, :]
    sine_part = jnp.sqrt(jnp.maximum(1.0 - cosine * cosine, 0.0))
    target = cosine * margin_cos - sine_part * margin_sin
    logits = logit_scale * jnp.where(positive, target, cosine)
    exp_terms = jnp.where(usable[None, :], jnp.exp(logits), jnp.float32(0.0))
    return (w_inv, w_unit, w_round, logits, exp_terms, positive)

def reference(features, centres, samples, counts, label_row, owner):
    values = features.astype(jnp.float32)
    col_mean = lax.optimization_barrier(jnp.mean(values, 0))
    centred = values - col_mean
    col_var = lax.optimization_barrier(jnp.mean(centred * centred, 0))
    inv_std = lax.rsqrt(col_var + epsilon)
    normed = centred * inv_std
    inv_norm = lax.rsqrt(lax.optimization_barrier(jnp.sum(normed * normed, 1)) + epsilon)
    unit_feats = normed * inv_norm[:, None]
    gathered = unit_feats.astype(jnp.bfloat16)
    blocks = centres.reshape(SHARDS, CEN_DEV, D)
    shard_ids = jnp.arange(SHARDS, dtype=jnp.int32)
    entries = (blocks, samples, counts, shard_ids)

    def first(running, entry):
        block, row_ids, live_count, shard_id = entry
        terms = shard_terms(gathered, block, row_ids, live_count, shard_id, label_row, owner)
        logits, exp_terms, positive = (terms[3], terms[4], terms[5])
        part_sum = lax.optimization_barrier(jnp.sum(exp_terms, 1))
        part_pos = lax.optimization_barrier(jnp.sum(jnp.where(positive, logits, jnp.float32(0.0)), 1))
        return ((running[0] + part_sum, running[1] + part_pos), None)
    start_sums = (jnp.zeros((IMAGES,), jnp.float32), jnp.zeros((IMAGES,), jnp.float32))
    (partition_sum, positive_logit), unused = lax.scan(first, start_sums, entries)
    loss = jnp.log(partition_sum) - positive_logit

    def second(accum_grad, entry):
        block, row_ids, live_count, shard_id = entry
        w_inv, w_unit, w_round, logits, exp_terms, positive = shard_terms(gathered, block, row_ids, live_count, shard_id, label_row, owner)
        grad_logit = logit_scale * (exp_terms / partition_sum[:, None] - positive.astype(jnp.float32))
        grad_round = grad_logit.astype(jnp.bfloat16).astype(jnp.float32)
        back_rows = jnp.dot(grad_round.T, gathered.astype(jnp.float32))
        radial_part = lax.optimization_barrier(jnp.sum(w_unit * back_rows, 1, keepdims=True))
        shard_grad = ((back_rows - w_unit * radial_part) * w_inv[:, None]).astype(jnp.bfloat16)
        accum_grad = accum_grad + jnp.dot(grad_round, w_round.astype(jnp.float32))
        return (accum_grad, shard_grad)
    grad_unit, centre_grad = lax.scan(second, jnp.zeros((IMAGES, D), jnp.float32), entries)
    radial_part = lax.optimization_barrier(jnp.sum(unit_feats * grad_unit, 1, keepdims=True))
    grad_normed = (grad_unit - unit_feats * radial_part) * inv_norm[:, None]
    grad_mean = lax.optimization_barrier(jnp.mean(grad_normed, 0))
    cross_mean = lax.optimization_barrier(jnp.mean(grad_normed * normed, 0))
    feature_grad = (grad_normed - grad_mean - normed * cross_mean) * inv_std
    return (feature_grad, centre_grad, loss)
```

```python
import functools
import math

import jax
import jax.numpy as jnp
from jax import lax
from jax.experimental import pallas as pl
from jax.experimental.pallas import tpu as pltpu
from jax.sharding import PartitionSpec as P

logit_scale = 64.0
margin_cos = math.cos(0.5)
margin_sin = math.sin(0.5)
epsilon = 1e-05

MESH = pl.DeviceIdType.MESH
f32 = jnp.float32
bf16 = jnp.bfloat16
L = 128
H = 256


def column(row):
    return jnp.transpose(jnp.broadcast_to(row, (L, L)))


def row_sum(block):
    return jnp.sum(jnp.transpose(block), axis=0, keepdims=True)


def margin_logit(cos):
    sine = jnp.sqrt(jnp.maximum(1.0 - cos * cos, 0.0))
    return logit_scale * (cos * margin_cos - sine * margin_sin)


def near_first(n):
    return sorted(range(1, n), key=lambda o: min(o, n - o))


def kernel(
    n, rows, images, slots, held,
    feat_ref, cen_hbm, samp_ref, count_ref, label_ref, owner_ref,
    fg_ref, cg_hbm, loss_ref,
    cen, picked, wround, wtrans, winv, labels, xbuf, feats, normed, inorm, ebuf, gbuf, qbuf,
    a_src, a_recv, pay, r1, r2, r3, fsend, drecv, csend, csum, crecv, bsrc, brecv, asrc, arecv, cgbuf,
    cen_sem, cg_sem, a_s, a_r, b_s, b_r, c_s, c_r, d_s, d_r, r1_s, r1_r, r2_s, r2_r, r3_s, r3_r,
    ds_s, ds_r, cs_s, cs_r, bs_s, bs_r, as_s, as_r,
):
    x = lax.axis_index("role")
    c = lax.axis_index("cls")
    k = c % 2
    t = c // 2
    y = t // n
    z = t % n
    a = y + (z - y) * k
    b = z + (y - z) * k
    step_a = 2 * n - (2 * n - 2) * k
    step_b = 2 + (2 * n - 2) * k
    other = c + 1 - 2 * k
    half = x // 2
    blocks = images // L
    ring = near_first(n)

    def along_a(o):
        return x, c + ((a + o) % n - a) * step_a

    def along_b(o):
        return x, c + ((b + o) % n - b) * step_b

    def remote(src, dst, send, recv, device):
        return pltpu.make_async_remote_copy(
            src_ref=src, dst_ref=dst, send_sem=send, recv_sem=recv, device_id=device, device_id_type=MESH
        )

    centre_copy = pltpu.make_async_copy(cen_hbm, cen, cen_sem)
    centre_copy.start()

    barrier = pltpu.get_barrier_semaphore()
    for o in range(1, n):
        for device in (along_a(o), along_b(o)):
            pl.semaphore_signal(barrier, inc=1, device_id=device, device_id_type=MESH)
    group = [((x + i // 2) % 4, c + (i % 2) * (1 - 2 * k)) for i in range(1, 8)]
    for device in group:
        pl.semaphore_signal(barrier, inc=1, device_id=device, device_id_type=MESH)
    a_src[...] = feat_ref[...].astype(f32)
    pl.semaphore_wait(barrier, 2 * (n - 1) + 7)

    def hop_one(i):
        return remote(
            a_src, a_recv.at[x % 2, k], a_s.at[i], a_r.at[(x % 2) * 2 + k], ((x + i) % 4, c - k + half)
        )

    for i in (1, 2, 3):
        hop_one(i).start()

    @pl.when(half != k)
    def _():
        hop_one(0).start()

    @pl.when(half == k)
    def _():
        a_recv[x % 2, k] = a_src[...]

    for j in range(2):
        for core in range(2):

            @pl.when(jnp.logical_or(2 * k + j != x, k != core))
            def _(j=j, core=core):
                remote(
                    a_src, a_recv.at[j, core], a_s.at[0], a_r.at[j * 2 + core], (x, other)
                ).wait_recv()

    tile = jnp.concatenate(
        [jnp.concatenate([a_recv[j, 0], a_recv[j, 1]], axis=0) for j in range(2)], axis=1
    )
    xbuf[k, y, z] = tile.astype(bf16)

    hop_two = {
        o: remote(xbuf.at[k, y, z], xbuf.at[k, y, z], b_s.at[o - 1], b_r.at[o - 1], along_a(o)) for o in ring
    }
    for o in ring:
        hop_two[o].start()

    shard = x * (2 * n * n) + c
    label_eff = jnp.where(owner_ref[...] == shard, label_ref[...], -1).astype(f32)
    for i in range(blocks):
        labels[i * L : (i + 1) * L, :] = column(label_eff[:, i * L : (i + 1) * L])
    slot = lax.broadcasted_iota(jnp.int32, (1, slots), 1)
    usable = slot < count_ref[0]
    slot_ids = jnp.where(usable, samp_ref[...], -2).astype(f32)
    slot_bias = jnp.where(usable, 0.0, -1e30).astype(f32)

    for o in ring:
        hop_two[o].wait_recv()

    def third(core):
        part = (lambda i: xbuf.at[0, :, i]) if core == 0 else (lambda i: xbuf.at[1, i])
        sends = {o: remote(part(b), part(b), c_s.at[o - 1], c_r.at[o - 1], along_b(o)) for o in ring}
        crosses = {
            o: remote(part((b - o) % n), part((b - o) % n), d_s.at[o], d_r.at[o], (x, other))
            for o in [0] + ring
        }
        return sends, crosses

    for core in range(2):

        @pl.when(k == core)
        def _(core=core):
            sends, crosses = third(core)
            for o in ring:
                sends[o].start()
            crosses[0].start()

    centre_copy.wait()
    lane = lax.broadcasted_iota(jnp.int32, (L, L), 1).astype(f32)

    def pick(i, carry):
        at = pl.ds(pl.multiple_of(i * L, L), L)
        ids = column(samp_ref[:, at].astype(f32))
        hot = [jnp.where(ids == lane + (j * L), 1.0, 0.0).astype(bf16) for j in range(held // L)]
        rows_f = jnp.dot(jnp.concatenate(hot, axis=1), cen[...], preferred_element_type=f32)
        picked[at, :] = rows_f.astype(bf16)
        inv = lax.rsqrt(jnp.sum(rows_f * rows_f, axis=1, keepdims=True) + epsilon)
        unit = rows_f * inv
        winv[at, :] = jnp.broadcast_to(inv, (L, L))
        wround[at, :] = unit.astype(bf16)
        wtrans[:, at] = jnp.transpose(unit).astype(bf16)
        return carry

    lax.fori_loop(0, slots // L, pick, 0)

    for core in range(2):

        @pl.when(k == core)
        def _(core=core):
            sends, crosses = third(core)
            for o in ring:
                sends[o].wait_recv()
                crosses[o].start()
            for o in [0] + ring:
                crosses[o].wait_recv()

    def part_of(h, i):
        return xbuf[h, i].reshape(n * rows, H).astype(f32)

    zero = jnp.zeros((1, H), f32)

    def add_up(i, sums):
        return tuple(sums[h] + jnp.sum(part_of(h, i), axis=0, keepdims=True) for h in range(2))

    mean = [s / images for s in lax.fori_loop(0, n, add_up, (zero, zero))]

    def add_squares(i, sums):
        out = []
        for h in range(2):
            centred = part_of(h, i) - mean[h]
            out.append(sums[h] + jnp.sum(centred * centred, axis=0, keepdims=True))
        return tuple(out)

    inv_std = [lax.rsqrt(s / images + epsilon) for s in lax.fori_loop(0, n, add_squares, (zero, zero))]

    m = n * rows

    def forward(i, carry):
        at = pl.ds(pl.multiple_of(i * m, m), m)
        norm = [(part_of(h, i) - mean[h]) * inv_std[h] for h in range(2)]
        squares = jnp.sum(norm[0] * norm[0], axis=1, keepdims=True) + jnp.sum(
            norm[1] * norm[1], axis=1, keepdims=True
        )
        inv = lax.rsqrt(squares + epsilon)
        inorm[at, :] = jnp.broadcast_to(inv, (m, L))
        unit = []
        for h in range(2):
            normed[h, at, :] = norm[h]
            unit.append((norm[h] * inv).astype(bf16))
        unit = jnp.concatenate(unit, axis=1)
        feats[at, :] = unit
        ebuf[at, :] = jnp.dot(unit, wtrans[...], preferred_element_type=f32)
        label = labels[at, :]
        cos_pos = jnp.zeros((m, L), f32)
        for j in range(slots // L):
            lanes = slice(j * L, (j + 1) * L)
            cos_pos += jnp.where(label == slot_ids[:, lanes], ebuf[at, lanes], 0.0)
        total = jnp.sum(cos_pos, axis=1, keepdims=True)
        pos_exp = jnp.broadcast_to(jnp.exp(margin_logit(total)), (m, L))
        sums = jnp.zeros((m, L), f32)
        for j in range(slots // L):
            lanes = slice(j * L, (j + 1) * L)
            plain = jnp.exp(logit_scale * ebuf[at, lanes] + slot_bias[:, lanes])
            term = jnp.where(label == slot_ids[:, lanes], pos_exp, plain)
            ebuf[at, lanes] = term
            sums += term
        pay[0:1, at] = row_sum(sums)
        pay[1:2, at] = row_sum(cos_pos)
        return carry

    lax.fori_loop(0, n, forward, 0)

    r1[a] = pay[...]
    stage = [remote(pay, r1.at[a], r1_s.at[o - 1], r1_r.at[o - 1], along_a(o)) for o in ring]
    for copy in stage:
        copy.start()
    for copy in stage:
        copy.wait()
    pay[...] = functools.reduce(lambda u, v: u + v, [r1[i] for i in range(n)])
    r2[b] = pay[...]
    stage = [remote(pay, r2.at[b], r2_s.at[o - 1], r2_r.at[o - 1], along_b(o)) for o in ring]
    for copy in stage:
        copy.start()
    for copy in stage:
        copy.wait()
    pay[...] = functools.reduce(lambda u, v: u + v, [r2[i] for i in range(n)])
    r3[x * 2 + k] = pay[...]
    stage = [remote(pay, r3.at[x * 2 + k], r3_s.at[i], r3_r.at[i], device) for i, device in enumerate(group)]
    for copy in stage:
        copy.start()
    for copy in stage:
        copy.wait()
    pay[...] = functools.reduce(lambda u, v: u + v, [r3[i] for i in range(8)])
    loss_ref[...] = jnp.log(pay[0:1, :]) - margin_logit(pay[1:2, :])
    pay[0:1, :] = logit_scale / pay[0:1, :]

    def backward(i, sums):
        at = pl.ds(pl.multiple_of(i * m, m), m)
        scale = jnp.transpose(jnp.broadcast_to(pay[0:1, at], (L, m)))
        label = labels[at, :]
        parts = []
        for j in range(slots // L):
            lanes = slice(j * L, (j + 1) * L)
            hit = jnp.where(label == slot_ids[:, lanes], logit_scale, 0.0)
            parts.append((ebuf[at, lanes] * scale - hit).astype(bf16))
        grad = jnp.concatenate(parts, axis=1)
        gbuf[at, :] = grad
        by_unit = jnp.dot(grad, wround[...], preferred_element_type=f32)
        by_unit = [by_unit[:, :H], by_unit[:, H:]]
        inv = inorm[at, :]
        inv = jnp.concatenate([inv, inv], axis=1)
        unit = [normed[h, at, :] * inv for h in range(2)]
        radial = jnp.sum(unit[0] * by_unit[0] + unit[1] * by_unit[1], axis=1, keepdims=True)
        out = []
        for h in range(2):
            q = (by_unit[h] - unit[h] * radial) * inv
            qbuf[h, i] = q.reshape(n, rows, H)
            out.append(sums[2 * h] + jnp.sum(q, axis=0, keepdims=True))
            out.append(sums[2 * h + 1] + jnp.sum(q * normed[h, at, :], axis=0, keepdims=True))
        return tuple(out)

    sums = lax.fori_loop(0, n, backward, (zero,) * 4)
    shift = [sums[0] / images, sums[2] / images]
    slope = [sums[1] / images, sums[3] / images]

    def pick_half(pair, mine):
        first = jnp.where(mine, k, 1 - k) == 0
        return jnp.where(first, pair[0], pair[1])

    def finish(h, i, mine):
        at = pl.ds(pl.multiple_of(i * m, m), m)
        q = qbuf[h, i].reshape(m, H)
        return (q - pick_half(shift, mine) - normed[h, at, :] * pick_half(slope, mine)) * pick_half(
            inv_std, mine
        )

    def theirs(i, carry):
        fsend[i] = finish(1 - k, i, False).reshape(n, rows, H).astype(bf16)
        return carry

    lax.fori_loop(0, n, theirs, 0)

    def reduce_hops(core):
        mine = (lambda i: drecv.at[:, i]) if core == 0 else (lambda i: drecv.at[i])
        cross_src = (lambda i: fsend.at[i]) if core == 0 else (lambda i: fsend.at[:, i])
        cross_dst = (lambda i: drecv.at[i]) if core == 0 else (lambda i: drecv.at[:, i])
        cross = [remote(cross_src(i), cross_dst(i), ds_s.at[i], ds_r.at[i], (x, other)) for i in range(n)]
        arrive = [remote(mine(i), mine(i), ds_s.at[i], ds_r.at[i], (x, other)) for i in range(n)]
        return cross, arrive

    for core in range(2):

        @pl.when(k == core)
        def _(core=core):
            for copy in reduce_hops(core)[0]:
                copy.start()

    def ours(i, carry):
        qbuf[k, i] = finish(k, i, True).reshape(n, rows, H)
        return carry

    lax.fori_loop(0, n, ours, 0)

    sends = {o: remote(csend.at[o - 1], crecv.at[o - 1], cs_s.at[o - 1], cs_r.at[o - 1], along_b(o)) for o in ring}
    for core in range(2):

        @pl.when(k == core)
        def _(core=core):
            for copy in reduce_hops(core)[1]:
                copy.wait_recv()

            def both(i):
                if core == 0:
                    return qbuf[0, :, i] + drecv[:, i].astype(f32)
                return qbuf[1, i] + drecv[i].astype(f32)

            for o in ring[::-1]:
                csend[o - 1] = both((b + o) % n).astype(bf16)
                sends[o].start()
            csum[...] = both(b)

    def by_centre(i, carry):
        at = pl.ds(pl.multiple_of(i * L, L), L)
        back = lax.dot_general(
            gbuf[:, at], feats[...], (((0,), (0,)), ((), ())), preferred_element_type=f32
        )
        inv = winv[at, :]
        inv = jnp.concatenate([inv] * (2 * H // L), axis=1)
        unit = picked[at, :].astype(f32) * inv
        radial = jnp.sum(unit * back, axis=1, keepdims=True)
        cgbuf[at, :] = ((back - unit * radial) * inv).astype(bf16)
        return carry

    lax.fori_loop(0, slots // L, by_centre, 0)
    out_copy = pltpu.make_async_copy(cgbuf, cg_hbm, cg_sem)
    out_copy.start()

    for o in ring:
        sends[o].wait_recv()
    for i in range(n):
        total = csum[i]
        for o in range(1, n):
            total += crecv[o - 1, i].astype(f32)
        bsrc[i] = total

    last = {
        o: remote(bsrc.at[(a + o) % n], brecv.at[o - 1], bs_s.at[o - 1], bs_r.at[o - 1], along_a(o)) for o in ring
    }
    for o in ring:
        last[o].start()
    for o in ring:
        last[o].wait_recv()
    total = bsrc[a]
    for o in range(1, n):
        total += brecv[o - 1]

    def hop_last(j, core):
        return remote(
            asrc.at[j, core], arecv.at[x], as_s.at[j * 2 + core], as_r.at[x], (2 * k + j, c - k + core)
        )

    for j in range(2):
        for core in range(2):
            asrc[j, core] = total[core * (rows // 2) : (core + 1) * (rows // 2), j * L : (j + 1) * L]
            mine = jnp.logical_and(2 * k + j == x, k == core)

            @pl.when(jnp.logical_not(mine))
            def _(j=j, core=core):
                hop_last(j, core).start()

            @pl.when(mine)
            def _(j=j, core=core):
                arecv[x] = asrc[j, core]

    for i in range(4):

        @pl.when(jnp.logical_or(x != i, half != k))
        def _(i=i):
            remote(asrc.at[0, 0], arecv.at[i], as_s.at[0], as_r.at[i], (x, other)).wait_recv()

    fg_ref[...] = (arecv[0] + arecv[1]) + (arecv[2] + arecv[3])

    for i in (1, 2, 3):
        hop_one(i).wait_send()

    @pl.when(half != k)
    def _():
        hop_one(0).wait_send()

    for o in ring:
        hop_two[o].wait_send()
        sends[o].wait_send()
        last[o].wait_send()
    for core in range(2):

        @pl.when(k == core)
        def _(core=core):
            first, crosses = third(core)
            for o in ring:
                first[o].wait_send()
            for o in [0] + ring:
                crosses[o].wait_send()
            for copy in reduce_hops(core)[0]:
                copy.wait_send()

    for j in range(2):
        for core in range(2):

            @pl.when(jnp.logical_or(2 * k + j != x, k != core))
            def _(j=j, core=core):
                hop_last(j, core).wait_send()

    out_copy.wait()


def body(n, features, centres, samples, counts, label_row, owner):
    rows = 2 * features.shape[0]
    images = label_row.shape[0]
    slots = samples.shape[1]
    held, width = centres.shape
    dma = pltpu.SemaphoreType.DMA
    vmem = pl.BlockSpec(memory_space=pltpu.VMEM)
    anywhere = pl.BlockSpec(memory_space=pl.ANY)
    feature_grad, centre_grad, loss_all = pl.pallas_call(
        functools.partial(kernel, n, rows, images, slots, held),
        out_shape=(
            jax.ShapeDtypeStruct(features.shape, f32),
            jax.ShapeDtypeStruct((slots, width), bf16),
            jax.ShapeDtypeStruct((1, images), f32),
        ),
        in_specs=[vmem, anywhere, vmem, pl.BlockSpec(memory_space=pltpu.SMEM), vmem, vmem],
        out_specs=(vmem, anywhere, vmem),
        scratch_shapes=[
            pltpu.VMEM((held, width), bf16),
            pltpu.VMEM((slots, width), bf16),
            pltpu.VMEM((slots, width), bf16),
            pltpu.VMEM((width, slots), bf16),
            pltpu.VMEM((slots, L), f32),
            pltpu.VMEM((images, L), f32),
            pltpu.VMEM((2, n, n, rows, H), bf16),
            pltpu.VMEM((images, width), bf16),
            pltpu.VMEM((2, images, H), f32),
            pltpu.VMEM((images, L), f32),
            pltpu.VMEM((images, slots), f32),
            pltpu.VMEM((images, slots), bf16),
            pltpu.VMEM((2, n, n, rows, H), f32),
            pltpu.VMEM((rows // 2, L), f32),
            pltpu.VMEM((2, 2, rows // 2, L), f32),
            pltpu.VMEM((2, images), f32),
            pltpu.VMEM((n, 2, images), f32),
            pltpu.VMEM((n, 2, images), f32),
            pltpu.VMEM((8, 2, images), f32),
            pltpu.VMEM((n, n, rows, H), bf16),
            pltpu.VMEM((n, n, rows, H), bf16),
            pltpu.VMEM((n - 1, n, rows, H), bf16),
            pltpu.VMEM((n, rows, H), f32),
            pltpu.VMEM((n - 1, n, rows, H), bf16),
            pltpu.VMEM((n, rows, H), f32),
            pltpu.VMEM((n - 1, rows, H), f32),
            pltpu.VMEM((2, 2, rows // 2, L), f32),
            pltpu.VMEM((4, rows // 2, L), f32),
            pltpu.VMEM((slots, width), bf16),
            dma(()), dma(()),
            dma((4,)), dma((4,)),
            dma((n - 1,)), dma((n - 1,)),
            dma((n - 1,)), dma((n - 1,)),
            dma((n,)), dma((n,)),
            dma((n - 1,)), dma((n - 1,)),
            dma((n - 1,)), dma((n - 1,)),
            dma((7,)), dma((7,)),
            dma((n,)), dma((n,)),
            dma((n - 1,)), dma((n - 1,)),
            dma((n - 1,)), dma((n - 1,)),
            dma((4,)), dma((4,)),
        ],
        compiler_params=pltpu.CompilerParams(
            collective_id=0, has_side_effects=True, vmem_limit_bytes=56 * 1024 * 1024
        ),
    )(features, centres, samples, counts, label_row[None], owner[None])
    own = features.shape[0]
    loss = lax.dynamic_slice_in_dim(loss_all[0], lax.axis_index("cls") * own, own, 0)
    return feature_grad, centre_grad[None], loss


def solution(mesh):
    n = math.isqrt(mesh.shape["cls"] // 2)
    return jax.shard_map(
        functools.partial(body, n),
        mesh=mesh,
        in_specs=(
            P("cls", "role"),
            P(("role", "cls"), None),
            P(("role", "cls"), None),
            P(("role", "cls")),
            P(),
            P(),
        ),
        out_specs=(P("cls", "role"), P(("role", "cls"), None, None), P("cls")),
        check_vma=False,
    )
```

```python
import functools
import math

import jax
import jax.numpy as jnp
from jax import lax
from jax.experimental import pallas as pl
from jax.experimental.pallas import tpu as pltpu
from jax.sharding import PartitionSpec as P

logit_scale = 64.0
margin_cos = math.cos(0.5)
margin_sin = math.sin(0.5)
epsilon = 1e-05

MESH = pl.DeviceIdType.MESH
f32 = jnp.float32
bf16 = jnp.bfloat16
L = 128


def column(row):
    return jnp.transpose(jnp.broadcast_to(row, (L, L)))


def row_sum(block):
    return jnp.sum(jnp.transpose(block), axis=0, keepdims=True)


def margin_logit(cos):
    sine = jnp.sqrt(jnp.maximum(1.0 - cos * cos, 0.0))
    return logit_scale * (cos * margin_cos - sine * margin_sin)


def wide(block, width):
    return jnp.concatenate([block] * (width // L), axis=1)


def add_all(ref, count):
    terms = [ref[i] for i in range(count)]
    while len(terms) > 1:
        terms = [terms[i] + terms[i + 1] for i in range(0, len(terms), 2)]
    return terms[0]


def kernel(
    n, roles, rows, slots, held,
    feat_hbm, cen_hbm, samp_hbm, count_hbm, label_hbm, owner_hbm,
    fg_hbm, cg_hbm, loss_hbm,
    feat, samp_row, ints, count, cen, picked, wround, wtrans, winv, labels, xbuf, feats, normed, inorm,
    ebuf, posexp, qn, qw, gbuf, qbuf, a_src, a_recv, part1, part2, cos1, cos2, scale,
    part1_in, part2_in, cos1_in, cos2_in, fsend, drecv, csend, csum, crecv, asrc, arecv, cgbuf, fg, loss,
    in_sem, out_sem, s1_s, s1_r, s2_s, s2_r, d_s, d_r, p1, p2, q1, q2, ds_s, ds_r, r2, r1,
):
    x = lax.axis_index("role")
    c = lax.axis_index("cls")
    k = c % 2
    t = c // 2
    y = t // n
    z = t % n
    width = L * roles
    own = rows // 2
    per = n // 2
    images = n * n * rows
    m = n * rows
    a = y + (z - y) * k
    b = z + (y - z) * k
    step_a = 2 * n - (2 * n - 2) * k
    step_b = 2 + (2 * n - 2) * k
    other = c + 1 - 2 * k
    q = (y + z) % 2
    aq = y + (z - y) * q
    step_q = 2 * n - (2 * n - 2) * q
    parity = (b + k) % 2
    self_one = k == q

    def remote(src, dst, send, recv, device):
        return pltpu.make_async_remote_copy(
            src_ref=src, dst_ref=dst, send_sem=send, recv_sem=recv, device_id=device, device_id_type=MESH
        )

    def wait_bytes(ref, sem):
        pltpu.make_async_copy(ref, ref, sem).wait()

    def far(o, size):
        return min(o, size - o)

    plane = [(i, o) for i in range(roles) for o in range(n)][1:]
    plane = sorted(plane, key=lambda p: -(far(p[0], roles) + far(p[1], n)))
    peers = len(plane)
    near = [sorted(range(p, n, 2), key=lambda o: far(o, n)) for p in range(2)]

    def in_plane(i, o):
        return (x + i) % roles, c + ((b + o) % n - b) * step_b

    barrier = pltpu.get_barrier_semaphore()

    def signal(device):
        pl.semaphore_signal(barrier, inc=1, device_id=device, device_id_type=MESH)

    def unless(condition, fn, *args):
        pl.when(jnp.logical_not(condition))(functools.partial(fn, *args))

    for i, o in plane:
        signal(in_plane(i, o))
    for core in range(2):
        at, step = (y, 2 * n) if core == 0 else (z, 2)
        for o in range(1, n):
            signal((x, c - k + core + ((at + o) % n - at) * step))
    signal((x, other))
    target_one = [(x, c - k + q + ((aq + o) % n - aq) * step_q) for o in range(n)]
    source_one = {
        (i, core): (x, c - k + core + (2 * i + parity - a) * step_a) for i in range(per) for core in range(2)
    }

    def is_me(i, core):
        return jnp.logical_and(2 * i + parity == a, k == core)

    for o in range(1, n):
        signal(target_one[o])
    unless(self_one, signal, target_one[0])
    for key in source_one:
        unless(is_me(*key), signal, source_one[key])

    feat_copy = pltpu.make_async_copy(feat_hbm, feat, in_sem.at[0])
    centre_copy = pltpu.make_async_copy(cen_hbm, cen, in_sem.at[1])
    count_copy = pltpu.make_async_copy(count_hbm, count, in_sem.at[2])
    int_copies = [
        pltpu.make_async_copy(src, dst, in_sem.at[3 + i])
        for i, (src, dst) in enumerate(((samp_hbm, samp_row), (label_hbm, ints.at[0]), (owner_hbm, ints.at[1])))
    ]
    for copy in (feat_copy, *int_copies, count_copy, centre_copy):
        copy.start()
    feat_copy.wait()
    a_src[...] = feat[...].astype(f32)
    for copy in int_copies:
        copy.wait()
    count_copy.wait()
    pl.semaphore_wait(barrier, peers + 4 * n - 1 - 2 * self_one.astype(jnp.int32))

    def hop_one(o):
        e = near[o % 2].index((n - o) % n)
        return remote(a_src, a_recv.at[e, k], s1_s, s1_r.at[e], target_one[o])

    for o in sorted(range(1, n), key=lambda o: -far(o, n)):
        hop_one(o).start()
    unless(self_one, lambda: hop_one(0).start())

    @pl.when(self_one)
    def _():
        a_recv[0, k] = a_src[...]

    shard = x * (2 * n * n) + c
    label_eff = jnp.where(ints[1] == shard, ints[0], -1).astype(f32)
    for i in range(images // L):
        labels[i * L : (i + 1) * L, :] = column(label_eff[:, i * L : (i + 1) * L])
    slot = lax.broadcasted_iota(jnp.int32, (1, slots), 1)
    usable = slot < count[0, 0]
    slot_ids = jnp.where(usable, samp_row[...], -2).astype(f32)
    slot_bias = jnp.where(usable, 0.0, -1e30).astype(f32)
    centre_copy.wait()

    lane = lax.broadcasted_iota(jnp.int32, (L, L), 1).astype(f32)

    def pick(i, carry):
        at = pl.ds(pl.multiple_of(i * L, L), L)
        ids = column(samp_row[:, at].astype(f32))
        hot = [jnp.where(ids == lane + (j * L), 1.0, 0.0).astype(bf16) for j in range(held // L)]
        rows_f = jnp.dot(jnp.concatenate(hot, axis=1), cen[...], preferred_element_type=f32)
        picked[at, :] = rows_f.astype(bf16)
        inv = lax.rsqrt(jnp.sum(rows_f * rows_f, axis=1, keepdims=True) + epsilon)
        unit = rows_f * inv
        winv[at, :] = jnp.broadcast_to(inv, (L, L))
        wround[at, :] = unit.astype(bf16)
        wtrans[:, at] = jnp.transpose(unit).astype(bf16)
        return carry

    blocks = slots // L
    cuts = [blocks * i // 8 for i in (0, 2, 3, 4, 5, 6, 7, 8)]

    def pick_some(i):
        if cuts[i] < cuts[i + 1]:
            lax.fori_loop(cuts[i], cuts[i + 1], pick, 0)

    pick_some(0)

    def tile_place(e):
        at = (a + jnp.where(self_one, near[0][e], near[1][e])) % n
        ty, tz = at + (y - at) * k, z + (at - z) * k
        return ty // 2, ty % 2, tz // 2, tz % 2

    def distance(i, o):
        return far(i, roles) + far(o, n)

    distances = sorted({distance(i, o) for i, o in plane})

    def hop_two(e, i, o):
        part = xbuf.at[(x, *tile_place(e))]
        return remote(part, part, s2_s, s2_r.at[distances.index(distance(i, o))], in_plane(i, o))

    for e in range(per):
        if e == 0:

            @pl.when(self_one)
            def _():
                wait_bytes(a_recv.at[0, 0], s1_r.at[0])

            unless(self_one, lambda: wait_bytes(a_recv.at[0], s1_r.at[0]))
        else:
            wait_bytes(a_recv.at[e], s1_r.at[e])
        xbuf[(x, *tile_place(e))] = jnp.concatenate([a_recv[e, 0], a_recv[e, 1]], axis=0).astype(bf16)
        for i, o in plane:
            hop_two(e, i, o).start()

    def tiles(ref, core, role, at):
        if core == 0:
            return ref.at[role, :, at % 2, at // 2, at % 2]
        return ref.at[role, at // 2, at % 2, :, (at + 1) % 2]

    def hop_three(core, i, o):
        part = tiles(xbuf, core, (x + roles - i) % roles, (b + n - o) % n)
        return remote(part, part, d_s, d_r, (x, other))

    def cross_part(members):
        for core in range(2):

            @pl.when(k == core)
            def _(core=core):
                for i, o in members:
                    hop_three(core, i, o).start()

    cross_part([(0, 0)])
    for e, dist in enumerate(distances):
        pick_some(1 + e)
        members = [p for p in plane if distance(*p) == dist]
        wait_bytes(csend.at[pl.ds(0, len(members))], s2_r.at[e])
        cross_part(members)
    for e in range(1 + len(distances), len(cuts) - 1):
        pick_some(e)
    wait_bytes(drecv.at[:, :, 0], d_r)

    def part_of(i):
        return jnp.concatenate(
            [xbuf[r, i // 2, i % 2].reshape(m, L).astype(f32) for r in range(roles)], axis=1
        )

    zero = jnp.zeros((1, width), f32)
    mean = lax.fori_loop(0, n, lambda i, s: s + jnp.sum(part_of(i), axis=0, keepdims=True), zero) / images

    def add_squares(i, s):
        centred = part_of(i) - mean
        return s + jnp.sum(centred * centred, axis=0, keepdims=True)

    inv_std = lax.rsqrt(lax.fori_loop(0, n, add_squares, zero) / images + epsilon)

    first_lane = lax.broadcasted_iota(jnp.int32, (m, L), 1) == 0

    def forward(i):
        at = slice(i * m, (i + 1) * m)
        norm = (part_of(i) - mean) * inv_std
        inv = lax.rsqrt(jnp.sum(norm * norm, axis=1, keepdims=True) + epsilon)
        inorm[at, :] = jnp.broadcast_to(inv, (m, L))
        normed[at, :] = norm
        unit = (norm * inv).astype(bf16)
        feats[at, :] = unit
        cosine = jnp.dot(unit, wtrans[...], preferred_element_type=f32)
        label = labels[at, :]
        cos_pos = jnp.zeros((m, L), f32)
        sums = jnp.zeros((m, L), f32)
        for j in range(slots // L):
            lanes = slice(j * L, (j + 1) * L)
            hit = label == slot_ids[:, lanes]
            cos = cosine[:, lanes]
            term = jnp.where(hit, 0.0, jnp.exp(logit_scale * cos + slot_bias[:, lanes]))
            ebuf[at, lanes] = term
            sums += term
            cos_pos += jnp.where(hit, cos, 0.0)
        total = jnp.sum(cos_pos, axis=1, keepdims=True)
        pos_exp = jnp.broadcast_to(jnp.exp(margin_logit(total)), (m, L))
        posexp[at, :] = pos_exp
        sums += jnp.where(jnp.logical_and(first_lane, label >= 0.0), pos_exp, 0.0)
        part1[i : i + 1, :] = row_sum(sums)
        cos1[i : i + 1, :] = row_sum(cos_pos)

    for i in range(n):
        forward(i)

    def sum_one(src, dst, sems, i, o):
        return remote(src, dst.at[x * n + b], sems.at[0], sems.at[1], in_plane(i, o))

    def sum_two(src, dst, sems, core, o):
        device = (x, c - k + core + ((a + o) % n - a) * step_a)
        return remote(src, dst.at[k * n + a], sems.at[0], sems.at[1], device)

    def each_two(src, dst, sems, act):
        for core in range(2):
            for o in range(1, n):
                act(sum_two(src, dst, sems, core, o))
        act(remote(src, dst.at[k * n + a], sems.at[0], sems.at[1], (x, other)))

    def start_one(src, dst, sems):
        dst[x * n + b] = src[...]
        for i, o in plane:
            sum_one(src, dst, sems, i, o).start()

    def finish_one(src, dst, sems, total):
        wait_bytes(dst.at[pl.ds(0, peers)], sems.at[1])
        total[...] = add_all(dst, roles * n)

    def start_two(src, dst, sems):
        dst[k * n + a] = src[...]
        each_two(src, dst, sems, lambda copy: copy.start())

    def finish_two(src, dst, sems):
        wait_bytes(dst.at[pl.ds(0, 2 * n - 1)], sems.at[1])
        return add_all(dst, 2 * n)

    part_one = (part1, part1_in, p1)
    part_two = (part2, part2_in, p2)
    cos_one = (cos1, cos1_in, q1)
    cos_two = (cos2, cos2_in, q2)
    start_one(*part_one)
    start_one(*cos_one)

    def by_terms(i, carry):
        at = pl.ds(pl.multiple_of(i * m, m), m)
        label = labels[at, :]
        hits = jnp.concatenate(
            [
                jnp.where(label == slot_ids[:, j * L : (j + 1) * L], 1.0, 0.0).astype(bf16)
                for j in range(slots // L)
            ],
            axis=1,
        )
        left = jnp.concatenate([ebuf[at, :].astype(bf16), hits], axis=0)
        both = jnp.dot(left, wround[...], preferred_element_type=f32)
        inv = wide(inorm[at, :], width)
        unit = normed[at, :] * inv
        for out, term in ((qn, both[:m]), (qw, both[m:])):
            radial = jnp.sum(unit * term, axis=1, keepdims=True)
            out[at, :] = (term - unit * radial) * inv
        return carry

    lax.fori_loop(0, n * 5 // 8, by_terms, 0)

    finish_one(*part_one, part2)
    start_two(*part_two)

    lax.fori_loop(n * 5 // 8, n, by_terms, 0)

    finish_one(*cos_one, cos2)
    start_two(*cos_two)

    total = finish_two(*part_two)
    log_sum = jnp.log(total)
    scale[...] = logit_scale / total

    def factors(i, at):
        plain = column(scale[pl.ds(i, 1), :])
        return plain, (posexp[at, :] * plain - logit_scale).astype(bf16).astype(f32)

    shift, slope = zero, zero
    for i in range(n):
        at = slice(i * m, (i + 1) * m)
        plain, hit = factors(i, at)
        value = qn[at, :] * wide(plain, width) + qw[at, :] * wide(hit, width)
        qn[at, :] = value
        shift += jnp.sum(value, axis=0, keepdims=True)
        slope += jnp.sum(value * normed[at, :], axis=0, keepdims=True)
    shift, slope = shift / images, slope / images

    def finish(i, carry):
        at = pl.ds(pl.multiple_of(i * m, m), m)
        value = (qn[at, :] - shift - normed[at, :] * slope) * inv_std
        for r in range(roles):
            tile = value[:, r * L : (r + 1) * L].reshape(n // 2, 2, rows, L)
            qbuf[r, i // 2, i % 2] = tile
            fsend[r, i // 2, i % 2] = tile.astype(bf16)
        return carry

    lax.fori_loop(0, n, finish, 0)

    def cross(core, i):
        every = pl.ds(0, roles)
        return remote(tiles(fsend, 1 - core, every, i), tiles(drecv, 1 - core, every, i), ds_s, ds_r.at[i], (x, other))

    for core in range(2):

        @pl.when(k == core)
        def _(core=core):
            for i in range(n):
                cross(core, i).start()

    def reduce_two(e, i, o):
        return remote(csend.at[e], crecv.at[e], r2.at[0], r2.at[1], in_plane(i, o))

    for i in range(n):
        wait_bytes(tiles(drecv, 0, pl.ds(0, roles), 0), ds_r.at[i])
    for core in range(2):

        @pl.when(k == core)
        def _(core=core):
            def both(role, at):
                return tiles(qbuf, core, role, at)[...] + tiles(drecv, core, role, at)[...].astype(f32)

            for e, (i, o) in enumerate(plane):
                csend[e] = both((x + i) % roles, (b + o) % n).astype(bf16)
                reduce_two(e, i, o).start()
            csum[...] = both(x, b)

    def logit_grad(i, carry):
        at = pl.ds(pl.multiple_of(i * m, m), m)
        plain, hit = factors(i, at)
        label = labels[at, :]
        for j in range(slots // L):
            lanes = slice(j * L, (j + 1) * L)
            gbuf[at, lanes] = jnp.where(label == slot_ids[:, lanes], hit, ebuf[at, lanes] * plain).astype(bf16)
        return carry

    lax.fori_loop(0, n, logit_grad, 0)

    def by_centre(i, carry):
        at = pl.ds(pl.multiple_of(i * L, L), L)
        back = lax.dot_general(gbuf[:, at], feats[...], (((0,), (0,)), ((), ())), preferred_element_type=f32)
        inv = wide(winv[at, :], width)
        unit = picked[at, :].astype(f32) * inv
        radial = jnp.sum(unit * back, axis=1, keepdims=True)
        cgbuf[at, :] = ((back - unit * radial) * inv).astype(bf16)
        return carry

    lax.fori_loop(0, slots // L, by_centre, 0)
    cg_copy = pltpu.make_async_copy(cgbuf, cg_hbm, out_sem.at[0])
    cg_copy.start()

    losses = log_sum - margin_logit(finish_two(*cos_two))
    row = lax.broadcasted_iota(jnp.int32, (n, L), 0)
    losses = jnp.sum(jnp.where(row == y, losses, 0.0), axis=0, keepdims=True)
    losses = pltpu.roll(jnp.broadcast_to(losses, (8, L)), (L - z * rows - k * own) % L, 1)
    loss[...] = losses[0:1, :own]
    loss_copy = pltpu.make_async_copy(loss, loss_hbm, out_sem.at[1])
    loss_copy.start()

    wait_bytes(crecv, r2.at[1])
    total = csum[...]
    for e in range(peers):
        total += crecv[e].astype(f32)

    def reduce_one(i, core):
        return remote(asrc.at[i, core], arecv.at[a], r1.at[0], r1.at[1], source_one[i, core])

    for i, core in source_one:
        asrc[i, core] = total[i, core * own : (core + 1) * own, :]
        unless(is_me(i, core), lambda i, core: reduce_one(i, core).start(), i, core)

        @pl.when(is_me(i, core))
        def _(i=i, core=core):
            arecv[a] = asrc[i, core]

    @pl.when(self_one)
    def _():
        wait_bytes(arecv.at[pl.ds(0, n - 1)], r1.at[1])

    unless(self_one, lambda: wait_bytes(arecv, r1.at[1]))
    fg[...] = add_all(arecv, n)
    fg_copy = pltpu.make_async_copy(fg, fg_hbm, out_sem.at[2])
    fg_copy.start()

    @pl.when(self_one)
    def _():
        wait_bytes(arecv.at[pl.ds(0, n - 1)], s1_s)
        wait_bytes(arecv.at[pl.ds(0, n - 1)], r1.at[0])

    @pl.when(jnp.logical_not(self_one))
    def _():
        wait_bytes(arecv, s1_s)
        wait_bytes(arecv, r1.at[0])

    wait_bytes(csend, s2_s)
    wait_bytes(drecv.at[:, :, 0], d_s)
    wait_bytes(drecv.at[:, :, 0], ds_s)
    wait_bytes(csend, r2.at[0])
    for sems in (p1, q1):
        wait_bytes(part1_in.at[pl.ds(0, peers)], sems.at[0])
    for sems in (p2, q2):
        wait_bytes(part2_in.at[pl.ds(0, 2 * n - 1)], sems.at[0])
    cg_copy.wait()
    loss_copy.wait()
    fg_copy.wait()


def hand_on(fg_in, cg_in, loss_in, fg_out, cg_out, loss_out, fg, cg, loss, sem):
    parts = 4
    size = cg_in.shape[0] // parts
    pairs = [(fg_in, fg, fg_out), (loss_in, loss, loss_out)]
    pairs += [tuple(ref.at[pl.ds(i * size, size)] for ref in (cg_in, cg, cg_out)) for i in range(parts)]
    ins = [pltpu.make_async_copy(src, mid, sem.at[i]) for i, (src, mid, _) in enumerate(pairs)]
    outs = [pltpu.make_async_copy(mid, dst, sem.at[i]) for i, (_, mid, dst) in enumerate(pairs)]
    for copy in ins:
        copy.start()
    for copy, out in zip(ins, outs):
        copy.wait()
        out.start()
    for out in outs:
        out.wait()


def body(n, roles, features, centres, samples, counts, label_row, owner):
    own = features.shape[0]
    rows = 2 * own
    images = label_row.shape[0]
    slots = samples.shape[1]
    held, width = centres.shape
    per = n // 2
    peers = roles * n - 1
    distances = roles // 2 + n // 2
    tiles = (roles, per, 2, per, 2, rows, L)
    dma = pltpu.SemaphoreType.DMA
    anywhere = pl.BlockSpec(memory_space=pl.ANY)
    hbm = pl.BlockSpec(memory_space=pltpu.HBM)
    out_shape = (
        jax.ShapeDtypeStruct(features.shape, f32),
        jax.ShapeDtypeStruct((slots, width), bf16),
        jax.ShapeDtypeStruct((1, own), f32),
    )
    results = pl.pallas_call(
        functools.partial(kernel, n, roles, rows, slots, held),
        out_shape=out_shape,
        in_specs=[hbm] * 6,
        out_specs=(anywhere,) * 3,
        scratch_shapes=[
            pltpu.VMEM(features.shape, bf16),
            pltpu.VMEM((1, slots), jnp.int32),
            pltpu.VMEM((2, 1, images), jnp.int32),
            pltpu.SMEM((1, 1), jnp.int32),
            pltpu.VMEM((held, width), bf16),
            pltpu.VMEM((slots, width), bf16),
            pltpu.VMEM((slots, width), bf16),
            pltpu.VMEM((width, slots), bf16),
            pltpu.VMEM((slots, L), f32),
            pltpu.VMEM((images, L), f32),
            pltpu.VMEM(tiles, bf16),
            pltpu.VMEM((images, width), bf16),
            pltpu.VMEM((images, width), f32),
            pltpu.VMEM((images, L), f32),
            pltpu.VMEM((images, slots), f32),
            pltpu.VMEM((images, L), f32),
            pltpu.VMEM((images, width), f32),
            pltpu.VMEM((images, width), f32),
            pltpu.VMEM((images, slots), bf16),
            pltpu.VMEM(tiles, f32),
            pltpu.VMEM((own, L), f32),
            pltpu.VMEM((per, 2, own, L), f32),
            pltpu.VMEM((n, L), f32),
            pltpu.VMEM((n, L), f32),
            pltpu.VMEM((n, L), f32),
            pltpu.VMEM((n, L), f32),
            pltpu.VMEM((n, L), f32),
            pltpu.VMEM((roles * n, n, L), f32),
            pltpu.VMEM((2 * n, n, L), f32),
            pltpu.VMEM((roles * n, n, L), f32),
            pltpu.VMEM((2 * n, n, L), f32),
            pltpu.VMEM(tiles, bf16),
            pltpu.VMEM(tiles, bf16),
            pltpu.VMEM((peers, per, rows, L), bf16),
            pltpu.VMEM((per, rows, L), f32),
            pltpu.VMEM((peers, per, rows, L), bf16),
            pltpu.VMEM((per, 2, own, L), f32),
            pltpu.VMEM((n, own, L), f32),
            pltpu.VMEM((slots, width), bf16),
            pltpu.VMEM((own, L), f32),
            pltpu.VMEM((1, own), f32),
            dma((6,)), dma((3,)),
            dma(()), dma((per,)),
            dma(()), dma((distances,)),
            dma(()), dma(()),
            dma((2,)), dma((2,)), dma((2,)), dma((2,)),
            dma(()), dma((n,)),
            dma((2,)), dma((2,)),
        ],
        compiler_params=pltpu.CompilerParams(
            collective_id=0, has_side_effects=True, vmem_limit_bytes=56 * 1024 * 1024
        ),
    )(features, centres, samples, counts[None], label_row[None], owner[None])
    feature_grad, centre_grad, loss = pl.pallas_call(
        hand_on,
        out_shape=out_shape,
        in_specs=[anywhere] * 3,
        out_specs=(anywhere,) * 3,
        scratch_shapes=[
            pltpu.VMEM(features.shape, f32), pltpu.VMEM((slots, width), bf16), pltpu.VMEM((1, own), f32), dma((6,))
        ],
    )(*results)
    return feature_grad, centre_grad[None], loss[0]


def solution(mesh):
    n = math.isqrt(mesh.shape["cls"] // 2)
    return jax.shard_map(
        functools.partial(body, n, mesh.shape["role"]),
        mesh=mesh,
        in_specs=(
            P("cls", "role"),
            P(("role", "cls"), None),
            P(("role", "cls"), None),
            P(("role", "cls")),
            P(),
            P(),
        ),
        out_specs=(P("cls", "role"), P(("role", "cls"), None, None), P("cls")),
        check_vma=False,
    )
```

```python
import functools
import math

import jax
import jax.numpy as jnp
from jax import lax
from jax.experimental import pallas as pl
from jax.experimental.pallas import tpu as pltpu
from jax.sharding import PartitionSpec as P

logit_scale = 64.0
margin_cos = math.cos(0.5)
margin_sin = math.sin(0.5)
epsilon = 1e-05

MESH = pl.DeviceIdType.MESH
f32 = jnp.float32
bf16 = jnp.bfloat16
L = 128


def column(row):
    return jnp.transpose(jnp.broadcast_to(row, (L, L)))


def row_sum(block):
    return jnp.sum(jnp.transpose(block), axis=0, keepdims=True)


def margin_logit(cos):
    sine = jnp.sqrt(jnp.maximum(1.0 - cos * cos, 0.0))
    return logit_scale * (cos * margin_cos - sine * margin_sin)


def wide(block, width):
    return jnp.concatenate([block] * (width // L), axis=1)


def add_all(ref, count):
    terms = [ref[i] for i in range(count)]
    while len(terms) > 1:
        terms = [terms[i] + terms[i + 1] for i in range(0, len(terms), 2)]
    return terms[0]


def kernel(
    n, roles, rows, slots, held,
    feat_hbm, cen_hbm, samp_hbm, count_hbm, label_hbm, owner_hbm,
    fg, cgbuf, loss,
    feat, samp_row, ints, count, cen, picked, wround, wtrans, winv, labels, xbuf, feats, normed, inorm,
    ebuf, posexp, qn, qw, gbuf, qbuf, a_src, a_recv, part1, part2, cos1, cos2, cosbuf, scale,
    part1_in, part2_in, cos1_in, cos2_in, fsend, drecv, csend, csum, crecv, asrc, arecv,
    in_sem, s1_s, s1_r, s2_s, s2_r, d_s, d_r, p1, p2, q1, q2, ds_s, ds_r, r2_s, r2_r, r1,
):
    x = lax.axis_index("role")
    c = lax.axis_index("cls")
    k = c % 2
    t = c // 2
    y = t // n
    z = t % n
    width = L * roles
    own = rows // 2
    per = n // 2
    images = n * n * rows
    m = n * rows
    a = y + (z - y) * k
    b = z + (y - z) * k
    step_a = 2 * n - (2 * n - 2) * k
    step_b = 2 + (2 * n - 2) * k
    other = c + 1 - 2 * k
    q = (y + z) % 2
    aq = y + (z - y) * q
    step_q = 2 * n - (2 * n - 2) * q
    parity = (b + k) % 2
    self_one = k == q

    def remote(src, dst, send, recv, device):
        return pltpu.make_async_remote_copy(
            src_ref=src, dst_ref=dst, send_sem=send, recv_sem=recv, device_id=device, device_id_type=MESH
        )

    def wait_bytes(ref, sem):
        pltpu.make_async_copy(ref, ref, sem).wait()

    def far(o, size):
        return min(o, size - o)

    plane = [(i, o) for i in range(roles) for o in range(n)][1:]
    plane = sorted(plane, key=lambda p: -(far(p[0], roles) + far(p[1], n)))
    peers = len(plane)
    near = [sorted(range(p, n, 2), key=lambda o: far(o, n)) for p in range(2)]

    def in_plane(i, o):
        return (x + i) % roles, c + ((b + o) % n - b) * step_b

    barrier = pltpu.get_barrier_semaphore()

    def signal(device):
        pl.semaphore_signal(barrier, inc=1, device_id=device, device_id_type=MESH)

    def unless(condition, fn, *args):
        pl.when(jnp.logical_not(condition))(functools.partial(fn, *args))

    for i, o in plane:
        signal(in_plane(i, o))
    for core in range(2):
        at, step = (y, 2 * n) if core == 0 else (z, 2)
        for o in range(1, n):
            signal((x, c - k + core + ((at + o) % n - at) * step))
    signal((x, other))
    target_one = [(x, c - k + q + ((aq + o) % n - aq) * step_q) for o in range(n)]
    source_one = {
        (i, core): (x, c - k + core + (2 * i + parity - a) * step_a) for i in range(per) for core in range(2)
    }

    def is_me(i, core):
        return jnp.logical_and(2 * i + parity == a, k == core)

    for o in range(1, n):
        signal(target_one[o])
    unless(self_one, signal, target_one[0])
    for key in source_one:
        unless(is_me(*key), signal, source_one[key])

    feat_copy = pltpu.make_async_copy(feat_hbm, feat, in_sem.at[0])
    centre_copy = pltpu.make_async_copy(cen_hbm, cen, in_sem.at[1])
    count_copy = pltpu.make_async_copy(count_hbm, count, in_sem.at[2])
    int_copies = [
        pltpu.make_async_copy(src, dst, in_sem.at[3 + i])
        for i, (src, dst) in enumerate(((samp_hbm, samp_row), (label_hbm, ints.at[0]), (owner_hbm, ints.at[1])))
    ]
    for copy in (feat_copy, *int_copies, count_copy, centre_copy):
        copy.start()
    feat_copy.wait()
    a_src[...] = feat[...].astype(f32)
    for copy in int_copies:
        copy.wait()
    count_copy.wait()
    pl.semaphore_wait(barrier, peers + 4 * n - 1 - 2 * self_one.astype(jnp.int32))

    def hop_one(o):
        e = near[o % 2].index((n - o) % n)
        return remote(a_src, a_recv.at[e, k], s1_s, s1_r.at[e], target_one[o])

    for o in sorted(range(1, n), key=lambda o: -far(o, n)):
        hop_one(o).start()
    unless(self_one, lambda: hop_one(0).start())

    @pl.when(self_one)
    def _():
        a_recv[0, k] = a_src[...]

    shard = x * (2 * n * n) + c
    label_eff = jnp.where(ints[1] == shard, ints[0], -1).astype(f32)
    for i in range(images // L):
        labels[i * L : (i + 1) * L, :] = column(label_eff[:, i * L : (i + 1) * L])
    slot = lax.broadcasted_iota(jnp.int32, (1, slots), 1)
    usable = slot < count[0, 0]
    slot_ids = jnp.where(usable, samp_row[...], -2).astype(f32)
    slot_bias = jnp.where(usable, 0.0, -1e30).astype(f32)
    centre_copy.wait()

    lane = lax.broadcasted_iota(jnp.int32, (L, L), 1).astype(f32)

    def pick(i, carry):
        at = pl.ds(pl.multiple_of(i * L, L), L)
        ids = column(samp_row[:, at].astype(f32))
        hot = [jnp.where(ids == lane + (j * L), 1.0, 0.0).astype(bf16) for j in range(held // L)]
        rows_f = jnp.dot(jnp.concatenate(hot, axis=1), cen[...], preferred_element_type=f32)
        picked[at, :] = rows_f.astype(bf16)
        inv = lax.rsqrt(jnp.sum(rows_f * rows_f, axis=1, keepdims=True) + epsilon)
        unit = rows_f * inv
        winv[at, :] = jnp.broadcast_to(inv, (L, L))
        wround[at, :] = unit.astype(bf16)
        wtrans[:, at] = jnp.transpose(unit).astype(bf16)
        return carry

    blocks = slots // L
    cuts = [blocks * i // 8 for i in (0, 1, 3, 4, 5, 6, 7, 8)]

    def pick_some(i):
        if cuts[i] < cuts[i + 1]:
            lax.fori_loop(cuts[i], cuts[i + 1], pick, 0)

    pick_some(0)

    def tile_place(e):
        at = (a + jnp.where(self_one, near[0][e], near[1][e])) % n
        ty, tz = at + (y - at) * k, z + (at - z) * k
        return ty // 2, ty % 2, tz // 2, tz % 2

    def distance(i, o):
        return far(i, roles) + far(o, n)

    distances = sorted({distance(i, o) for i, o in plane})

    def hop_two(e, i, o):
        part = xbuf.at[(x, *tile_place(e))]
        return remote(part, part, s2_s, s2_r.at[distances.index(distance(i, o))], in_plane(i, o))

    for e in range(per):
        if e == 0:

            @pl.when(self_one)
            def _():
                wait_bytes(a_recv.at[0, 0], s1_r.at[0])

            unless(self_one, lambda: wait_bytes(a_recv.at[0], s1_r.at[0]))
        else:
            wait_bytes(a_recv.at[e], s1_r.at[e])
        xbuf[(x, *tile_place(e))] = jnp.concatenate([a_recv[e, 0], a_recv[e, 1]], axis=0).astype(bf16)
        for i, o in plane:
            hop_two(e, i, o).start()

    def tiles(ref, core, role, at):
        if core == 0:
            return ref.at[role, :, at % 2, at // 2, at % 2]
        return ref.at[role, at // 2, at % 2, :, (at + 1) % 2]

    def hop_three(core, i, o):
        part = tiles(xbuf, core, (x + roles - i) % roles, (b + n - o) % n)
        return remote(part, part, d_s, d_r, (x, other))

    def cross_part(members):
        for core in range(2):

            @pl.when(k == core)
            def _(core=core):
                for i, o in members:
                    hop_three(core, i, o).start()

    cross_part([(0, 0)])
    for e, dist in enumerate(distances):
        pick_some(1 + e)
        members = [p for p in plane if distance(*p) == dist]
        wait_bytes(csend.at[:, pl.ds(0, len(members))], s2_r.at[e])
        cross_part(members)
    for e in range(1 + len(distances), len(cuts) - 1):
        pick_some(e)
    wait_bytes(drecv.at[:, :, 0], d_r)

    def part_of(i):
        return jnp.concatenate(
            [xbuf[r, i // 2, i % 2].reshape(m, L).astype(f32) for r in range(roles)], axis=1
        )

    zero = jnp.zeros((1, width), f32)
    mean = lax.fori_loop(0, n, lambda i, s: s + jnp.sum(part_of(i), axis=0, keepdims=True), zero) / images

    def add_squares(i, s):
        centred = part_of(i) - mean
        return s + jnp.sum(centred * centred, axis=0, keepdims=True)

    inv_std = lax.rsqrt(lax.fori_loop(0, n, add_squares, zero) / images + epsilon)

    first_lane = lax.broadcasted_iota(jnp.int32, (m, L), 1) == 0

    def forward(i):
        at = slice(i * m, (i + 1) * m)
        norm = (part_of(i) - mean) * inv_std
        inv = lax.rsqrt(jnp.sum(norm * norm, axis=1, keepdims=True) + epsilon)
        inorm[at, :] = jnp.broadcast_to(inv, (m, L))
        normed[at, :] = norm
        unit = (norm * inv).astype(bf16)
        feats[at, :] = unit
        cosine = jnp.dot(unit, wtrans[...], preferred_element_type=f32)
        label = labels[at, :]
        cos_pos = jnp.zeros((m, L), f32)
        sums = jnp.zeros((m, L), f32)
        for j in range(slots // L):
            lanes = slice(j * L, (j + 1) * L)
            hit = label == slot_ids[:, lanes]
            cos = cosine[:, lanes]
            term = jnp.where(hit, 0.0, jnp.exp(logit_scale * cos + slot_bias[:, lanes]))
            ebuf[at, lanes] = term
            sums += term
            cos_pos += jnp.where(hit, cos, 0.0)
        total = jnp.sum(cos_pos, axis=1, keepdims=True)
        pos_exp = jnp.broadcast_to(jnp.exp(margin_logit(total)), (m, L))
        posexp[at, :] = pos_exp
        sums += jnp.where(jnp.logical_and(first_lane, label >= 0.0), pos_exp, 0.0)
        part1[i : i + 1, :] = row_sum(sums)
        cosbuf[at, :] = cos_pos

    for i in range(n):
        forward(i)

    def sum_one(src, dst, sems, i, o):
        return remote(src, dst.at[x * n + b], sems.at[0], sems.at[1], in_plane(i, o))

    def sum_two(src, dst, sems, core, o):
        device = (x, c - k + core + ((a + o) % n - a) * step_a)
        return remote(src, dst.at[k * n + a], sems.at[0], sems.at[1], device)

    def each_two(src, dst, sems, act):
        for core in range(2):
            for o in range(1, n):
                act(sum_two(src, dst, sems, core, o))
        act(remote(src, dst.at[k * n + a], sems.at[0], sems.at[1], (x, other)))

    def start_one(src, dst, sems):
        dst[x * n + b] = src[...]
        for i, o in plane:
            sum_one(src, dst, sems, i, o).start()

    def finish_one(src, dst, sems, total):
        wait_bytes(dst.at[pl.ds(0, peers)], sems.at[1])
        total[...] = add_all(dst, roles * n)

    def start_two(src, dst, sems):
        dst[k * n + a] = src[...]
        each_two(src, dst, sems, lambda copy: copy.start())

    def finish_two(src, dst, sems):
        wait_bytes(dst.at[pl.ds(0, 2 * n - 1)], sems.at[1])
        return add_all(dst, 2 * n)

    part_one = (part1, part1_in, p1)
    part_two = (part2, part2_in, p2)
    cos_one = (cos1, cos1_in, q1)
    cos_two = (cos2, cos2_in, q2)
    start_one(*part_one)
    for i in range(n):
        cos1[i : i + 1, :] = row_sum(cosbuf[i * m : (i + 1) * m, :])
    start_one(*cos_one)

    def by_terms(i, carry):
        at = pl.ds(pl.multiple_of(i * m, m), m)
        label = labels[at, :]
        hits = jnp.concatenate(
            [
                jnp.where(label == slot_ids[:, j * L : (j + 1) * L], 1.0, 0.0).astype(bf16)
                for j in range(slots // L)
            ],
            axis=1,
        )
        left = jnp.concatenate([ebuf[at, :].astype(bf16), hits], axis=0)
        both = jnp.dot(left, wround[...], preferred_element_type=f32)
        inv = wide(inorm[at, :], width)
        unit = normed[at, :] * inv
        for out, term in ((qn, both[:m]), (qw, both[m:])):
            radial = jnp.sum(unit * term, axis=1, keepdims=True)
            out[at, :] = (term - unit * radial) * inv
        return carry

    lax.fori_loop(0, n * 5 // 8, by_terms, 0)

    finish_one(*part_one, part2)
    start_two(*part_two)

    lax.fori_loop(n * 5 // 8, n, by_terms, 0)

    total = finish_two(*part_two)
    log_sum = jnp.log(total)
    scale[...] = logit_scale / total

    def factors(i, at):
        plain = column(scale[pl.ds(i, 1), :])
        return plain, (posexp[at, :] * plain - logit_scale).astype(bf16).astype(f32)

    shift, slope = zero, zero
    for i in range(n):
        at = slice(i * m, (i + 1) * m)
        plain, hit = factors(i, at)
        value = qn[at, :] * wide(plain, width) + qw[at, :] * wide(hit, width)
        qn[at, :] = value
        shift += jnp.sum(value, axis=0, keepdims=True)
        slope += jnp.sum(value * normed[at, :], axis=0, keepdims=True)
    shift, slope = shift / images, slope / images

    def finish(core, out):
        def block(i, carry):
            p = (i + core) % 2
            for j in range(per):
                at = pl.ds(pl.multiple_of(i * m + (2 * j + p) * rows, rows), rows)
                value = (qn[at, :] - shift - normed[at, :] * slope) * inv_std
                for r in range(roles):
                    out[r, i // 2, i % 2, j, p] = value[:, r * L : (r + 1) * L].astype(out.dtype)
            return carry

        lax.fori_loop(0, n, block, 0)

    finish(1 - k, fsend)

    by_far = sorted(range(n), key=lambda o: -far(o, n))

    def cross(core, i):
        every = pl.ds(0, roles)
        return remote(
            tiles(fsend, 1 - core, every, i), tiles(drecv, 1 - core, every, i), ds_s, ds_r.at[i], (x, other)
        )

    for core in range(2):

        @pl.when(k == core)
        def _(core=core):
            for o in by_far:
                cross(core, (a + o) % n).start()

    finish(k, qbuf)

    def tile_of(at, e):
        return ((a + jnp.where((a + at + k) % 2 == 0, near[0][e], near[1][e])) % n) // 2

    def reduce_two(e, f, i, o):
        return remote(csend.at[e, f], crecv.at[e, f], r2_s, r2_r.at[e], in_plane(i, o))

    arrived = set()

    def cross_wait(o):
        if o not in arrived:
            arrived.add(o)
            wait_bytes(tiles(drecv, 0, pl.ds(0, roles), 0), ds_r.at[(b + o) % n])

    def both(e, role, at):
        i = tile_of(at, e)
        ay, by = i, at // 2
        pa, pb = (at + k) % 2, at % 2
        place = (role, ay + (by - ay) * k, pa + (pb - pa) * k, by + (ay - by) * k, pb + (pa - pb) * k)
        return qbuf[place] + drecv[place].astype(f32)

    for e in reversed(range(per)):
        for f, (i, o) in enumerate(plane):
            cross_wait(o)
            csend[e, f] = both(e, (x + i) % roles, (b + o) % n).astype(bf16)
            reduce_two(e, f, i, o).start()
        cross_wait(0)
        csum[e] = both(e, x, b)

    finish_one(*cos_one, cos2)
    start_two(*cos_two)

    def logit_grad(i, carry):
        at = pl.ds(pl.multiple_of(i * m, m), m)
        plain, hit = factors(i, at)
        label = labels[at, :]
        for j in range(slots // L):
            lanes = slice(j * L, (j + 1) * L)
            gbuf[at, lanes] = jnp.where(label == slot_ids[:, lanes], hit, ebuf[at, lanes] * plain).astype(bf16)
        return carry

    lax.fori_loop(0, n, logit_grad, 0)

    def by_centre(i, carry):
        at = pl.ds(pl.multiple_of(i * L, L), L)
        back = lax.dot_general(gbuf[:, at], feats[...], (((0,), (0,)), ((), ())), preferred_element_type=f32)
        inv = wide(winv[at, :], width)
        unit = picked[at, :].astype(f32) * inv
        radial = jnp.sum(unit * back, axis=1, keepdims=True)
        cgbuf[at, :] = ((back - unit * radial) * inv).astype(bf16)
        return carry

    lax.fori_loop(0, slots // L, by_centre, 0)

    losses = log_sum - margin_logit(finish_two(*cos_two))
    row = lax.broadcasted_iota(jnp.int32, (n, L), 0)
    losses = jnp.sum(jnp.where(row == y, losses, 0.0), axis=0, keepdims=True)
    losses = pltpu.roll(jnp.broadcast_to(losses, (8, L)), (L - z * rows - k * own) % L, 1)
    loss[...] = losses[0:1, :own]

    def reduce_one(e, core):
        device = (x, c - k + core + ((a + jnp.where(self_one, near[0][e], near[1][e])) % n - a) * step_a)
        return remote(asrc.at[e, core], arecv.at[a], r1.at[0], r1.at[1], device)

    for e in reversed(range(per)):
        wait_bytes(crecv.at[e], r2_r.at[e])
        terms = [csum[e]] + [crecv[e, f].astype(f32) for f in range(peers)]
        while len(terms) > 1:
            terms = [terms[i] + terms[i + 1] for i in range(0, len(terms), 2)]
        for core in range(2):
            asrc[e, core] = terms[0][core * own : (core + 1) * own, :]
        if e:
            for core in range(2):
                reduce_one(e, core).start()
        else:
            for core in range(2):
                me = jnp.logical_and(self_one, k == core)
                unless(me, lambda core: reduce_one(0, core).start(), core)

                @pl.when(me)
                def _(core=core):
                    arecv[a] = asrc[0, core]

    @pl.when(self_one)
    def _():
        wait_bytes(arecv.at[pl.ds(0, n - 1)], r1.at[1])

    unless(self_one, lambda: wait_bytes(arecv, r1.at[1]))
    fg[...] = add_all(arecv, n)

    @pl.when(self_one)
    def _():
        wait_bytes(arecv.at[pl.ds(0, n - 1)], s1_s)
        wait_bytes(arecv.at[pl.ds(0, n - 1)], r1.at[0])

    @pl.when(jnp.logical_not(self_one))
    def _():
        wait_bytes(arecv, s1_s)
        wait_bytes(arecv, r1.at[0])

    wait_bytes(csend, s2_s)
    wait_bytes(drecv.at[:, :, 0], d_s)
    wait_bytes(drecv.at[:, :, 0], ds_s)
    wait_bytes(csend, r2_s)
    for sems in (p1, q1):
        wait_bytes(part1_in.at[pl.ds(0, peers)], sems.at[0])
    for sems in (p2, q2):
        wait_bytes(part2_in.at[pl.ds(0, 2 * n - 1)], sems.at[0])


def hand_on(fg_in, cg_in, loss_in, fg_out, cg_out, loss_out, sem):
    parts = 8
    size = cg_in.shape[0] // parts
    pairs = [(fg_in, fg_out), (loss_in, loss_out)]
    pairs += [tuple(ref.at[pl.ds(i * size, size)] for ref in (cg_in, cg_out)) for i in range(parts)]
    copies = [pltpu.make_async_copy(src, dst, sem.at[i]) for i, (src, dst) in enumerate(pairs)]
    for copy in copies:
        copy.start()
    for copy in copies:
        copy.wait()


def body(n, roles, features, centres, samples, counts, label_row, owner):
    own = features.shape[0]
    rows = 2 * own
    images = label_row.shape[0]
    slots = samples.shape[1]
    held, width = centres.shape
    per = n // 2
    peers = roles * n - 1
    distances = roles // 2 + n // 2
    tiles = (roles, per, 2, per, 2, rows, L)
    dma = pltpu.SemaphoreType.DMA
    anywhere = pl.BlockSpec(memory_space=pl.ANY)
    vmem = pl.BlockSpec(memory_space=pltpu.VMEM)
    hbm = pl.BlockSpec(memory_space=pltpu.HBM)
    out_shape = (
        jax.ShapeDtypeStruct(features.shape, f32),
        jax.ShapeDtypeStruct((slots, width), bf16),
        jax.ShapeDtypeStruct((1, own), f32),
    )
    results = pl.pallas_call(
        functools.partial(kernel, n, roles, rows, slots, held),
        out_shape=tuple(pltpu.VMEM(s.shape, s.dtype) for s in out_shape),
        in_specs=[hbm] * 6,
        out_specs=(vmem,) * 3,
        scratch_shapes=[
            pltpu.VMEM(features.shape, bf16),
            pltpu.VMEM((1, slots), jnp.int32),
            pltpu.VMEM((2, 1, images), jnp.int32),
            pltpu.SMEM((1, 1), jnp.int32),
            pltpu.VMEM((held, width), bf16),
            pltpu.VMEM((slots, width), bf16),
            pltpu.VMEM((slots, width), bf16),
            pltpu.VMEM((width, slots), bf16),
            pltpu.VMEM((slots, L), f32),
            pltpu.VMEM((images, L), f32),
            pltpu.VMEM(tiles, bf16),
            pltpu.VMEM((images, width), bf16),
            pltpu.VMEM((images, width), f32),
            pltpu.VMEM((images, L), f32),
            pltpu.VMEM((images, slots), f32),
            pltpu.VMEM((images, L), f32),
            pltpu.VMEM((images, width), f32),
            pltpu.VMEM((images, width), f32),
            pltpu.VMEM((images, slots), bf16),
            pltpu.VMEM(tiles, f32),
            pltpu.VMEM((own, L), f32),
            pltpu.VMEM((per, 2, own, L), f32),
            pltpu.VMEM((n, L), f32),
            pltpu.VMEM((n, L), f32),
            pltpu.VMEM((n, L), f32),
            pltpu.VMEM((n, L), f32),
            pltpu.VMEM((images, L), f32),
            pltpu.VMEM((n, L), f32),
            pltpu.VMEM((roles * n, n, L), f32),
            pltpu.VMEM((2 * n, n, L), f32),
            pltpu.VMEM((roles * n, n, L), f32),
            pltpu.VMEM((2 * n, n, L), f32),
            pltpu.VMEM(tiles, bf16),
            pltpu.VMEM(tiles, bf16),
            pltpu.VMEM((per, peers, rows, L), bf16),
            pltpu.VMEM((per, rows, L), f32),
            pltpu.VMEM((per, peers, rows, L), bf16),
            pltpu.VMEM((per, 2, own, L), f32),
            pltpu.VMEM((n, own, L), f32),
            dma((6,)),
            dma(()), dma((per,)),
            dma(()), dma((distances,)),
            dma(()), dma(()),
            dma((2,)), dma((2,)), dma((2,)), dma((2,)),
            dma(()), dma((n,)),
            dma(()), dma((per,)),
            dma((2,)),
        ],
        compiler_params=pltpu.CompilerParams(
            collective_id=0, has_side_effects=True, vmem_limit_bytes=56 * 1024 * 1024
        ),
    )(features, centres, samples, counts[None], label_row[None], owner[None])
    feature_grad, centre_grad, loss = pl.pallas_call(
        hand_on,
        out_shape=out_shape,
        in_specs=[vmem] * 3,
        out_specs=(anywhere,) * 3,
        scratch_shapes=[dma((10,))],
    )(*(pltpu.with_memory_space_constraint(r, pltpu.VMEM) for r in results))
    return feature_grad, centre_grad[None], loss[0]


def solution(mesh):
    n = math.isqrt(mesh.shape["cls"] // 2)
    return jax.shard_map(
        functools.partial(body, n, mesh.shape["role"]),
        mesh=mesh,
        in_specs=(
            P("cls", "role"),
            P(("role", "cls"), None),
            P(("role", "cls"), None),
            P(("role", "cls")),
            P(),
            P(),
        ),
        out_specs=(P("cls", "role"), P(("role", "cls"), None, None), P("cls")),
        check_vma=False,
    )
```

```python
import functools
import math

import jax
import jax.numpy as jnp
from jax import lax
from jax.experimental import pallas as pl
from jax.experimental.pallas import tpu as pltpu
from jax.sharding import PartitionSpec as P

logit_scale = 64.0
margin_cos = math.cos(0.5)
margin_sin = math.sin(0.5)
epsilon = 1e-05

MESH = pl.DeviceIdType.MESH
f32 = jnp.float32
bf16 = jnp.bfloat16
L = 128


def column(row):
    return jnp.transpose(jnp.broadcast_to(row, (L, L)))


def row_sum(block):
    return jnp.sum(jnp.transpose(block), axis=0, keepdims=True)


def margin_logit(cos):
    sine = jnp.sqrt(jnp.maximum(1.0 - cos * cos, 0.0))
    return logit_scale * (cos * margin_cos - sine * margin_sin)


def wide(block, width):
    return jnp.concatenate([block] * (width // L), axis=1)


def add_all(ref, count):
    terms = [ref[i] for i in range(count)]
    while len(terms) > 1:
        terms = [terms[i] + terms[i + 1] for i in range(0, len(terms), 2)]
    return terms[0]


def kernel(
    n, roles, rows, slots, held,
    feat_hbm, cen_hbm, samp_hbm, count_hbm, label_hbm, owner_hbm,
    fg, cgbuf, loss,
    feat, samp_row, ints, count, cen, picked, wround, wtrans, winv, labels, xbuf, feats, normed, inorm,
    ebuf, posexp, qn, qw, gbuf, qbuf, a_src, a_recv, part1, part2, cos1, cos2, cosbuf, scale,
    part1_in, part2_in, cos1_in, cos2_in, fsend, drecv, csend, csum, crecv, asrc, arecv,
    in_sem, s1_s, s1_r, s2_s, s2_r, d_s, d_r, p1, p2, q1, q2, ds_s, ds_r, r2_s, r2_r, r1,
):
    x = lax.axis_index("role")
    c = lax.axis_index("cls")
    k = c % 2
    t = c // 2
    y = t // n
    z = t % n
    width = L * roles
    own = rows // 2
    per = n // 2
    images = n * n * rows
    m = n * rows
    a = y + (z - y) * k
    b = z + (y - z) * k
    step_a = 2 * n - (2 * n - 2) * k
    step_b = 2 + (2 * n - 2) * k
    other = c + 1 - 2 * k
    q = (y + z) % 2
    aq = y + (z - y) * q
    step_q = 2 * n - (2 * n - 2) * q
    parity = (b + k) % 2
    self_one = k == q

    def remote(src, dst, send, recv, device):
        return pltpu.make_async_remote_copy(
            src_ref=src, dst_ref=dst, send_sem=send, recv_sem=recv, device_id=device, device_id_type=MESH
        )

    def wait_bytes(ref, sem):
        pltpu.make_async_copy(ref, ref, sem).wait()

    def far(o, size):
        return min(o, size - o)

    plane = [(i, o) for i in range(roles) for o in range(n)][1:]
    plane = sorted(plane, key=lambda p: -(far(p[0], roles) + far(p[1], n)))
    peers = len(plane)
    near = [sorted(range(p, n, 2), key=lambda o: far(o, n)) for p in range(2)]

    def in_plane(i, o):
        return (x + i) % roles, c + ((b + o) % n - b) * step_b

    barrier = pltpu.get_barrier_semaphore()

    def signal(device):
        pl.semaphore_signal(barrier, inc=1, device_id=device, device_id_type=MESH)

    def unless(condition, fn, *args):
        pl.when(jnp.logical_not(condition))(functools.partial(fn, *args))

    for i, o in plane:
        signal(in_plane(i, o))
    for core in range(2):
        at, step = (y, 2 * n) if core == 0 else (z, 2)
        for o in range(1, n):
            signal((x, c - k + core + ((at + o) % n - at) * step))
    signal((x, other))
    target_one = [(x, c - k + q + ((aq + o) % n - aq) * step_q) for o in range(n)]
    source_one = {
        (i, core): (x, c - k + core + (2 * i + parity - a) * step_a) for i in range(per) for core in range(2)
    }

    def is_me(i, core):
        return jnp.logical_and(2 * i + parity == a, k == core)

    for o in range(1, n):
        signal(target_one[o])
    unless(self_one, signal, target_one[0])
    for key in source_one:
        unless(is_me(*key), signal, source_one[key])

    feat_copy = pltpu.make_async_copy(feat_hbm, feat, in_sem.at[0])
    centre_copy = pltpu.make_async_copy(cen_hbm, cen, in_sem.at[1])
    count_copy = pltpu.make_async_copy(count_hbm, count, in_sem.at[2])
    int_copies = [
        pltpu.make_async_copy(src, dst, in_sem.at[3 + i])
        for i, (src, dst) in enumerate(((samp_hbm, samp_row), (label_hbm, ints.at[0]), (owner_hbm, ints.at[1])))
    ]
    for copy in (feat_copy, *int_copies, count_copy, centre_copy):
        copy.start()
    feat_copy.wait()
    a_src[...] = feat[...].astype(f32)
    for copy in int_copies:
        copy.wait()
    count_copy.wait()
    pl.semaphore_wait(barrier, peers + 4 * n - 1 - 2 * self_one.astype(jnp.int32))

    def hop_one(o):
        e = near[o % 2].index((n - o) % n)
        return remote(a_src, a_recv.at[e, k], s1_s, s1_r.at[e], target_one[o])

    for o in sorted(range(1, n), key=lambda o: -far(o, n)):
        hop_one(o).start()
    unless(self_one, lambda: hop_one(0).start())

    @pl.when(self_one)
    def _():
        a_recv[0, k] = a_src[...]

    shard = x * (2 * n * n) + c
    label_eff = jnp.where(ints[1] == shard, ints[0], -1).astype(f32)
    for i in range(images // L):
        labels[i * L : (i + 1) * L, :] = column(label_eff[:, i * L : (i + 1) * L])
    slot = lax.broadcasted_iota(jnp.int32, (1, slots), 1)
    usable = slot < count[0, 0]
    slot_ids = jnp.where(usable, samp_row[...], -2).astype(f32)
    slot_bias = jnp.where(usable, 0.0, -1e30).astype(f32)
    centre_copy.wait()

    lane = lax.broadcasted_iota(jnp.int32, (L, L), 1).astype(f32)

    def pick(i, carry):
        at = pl.ds(pl.multiple_of(i * L, L), L)
        ids = column(samp_row[:, at].astype(f32))
        hot = [jnp.where(ids == lane + (j * L), 1.0, 0.0).astype(bf16) for j in range(held // L)]
        rows_f = jnp.dot(jnp.concatenate(hot, axis=1), cen[...], preferred_element_type=f32)
        picked[at, :] = rows_f.astype(bf16)
        inv = lax.rsqrt(jnp.sum(rows_f * rows_f, axis=1, keepdims=True) + epsilon)
        unit = rows_f * inv
        winv[at, :] = jnp.broadcast_to(inv, (L, L))
        wround[at, :] = unit.astype(bf16)
        wtrans[:, at] = jnp.transpose(unit).astype(bf16)
        return carry

    blocks = slots // L
    cuts = [blocks * i // 8 for i in (0, 1, 3, 4, 5, 6, 7, 8)]

    def pick_some(i):
        if cuts[i] < cuts[i + 1]:
            lax.fori_loop(cuts[i], cuts[i + 1], pick, 0)

    pick_some(0)

    def tile_place(e):
        at = (a + jnp.where(self_one, near[0][e], near[1][e])) % n
        ty, tz = at + (y - at) * k, z + (at - z) * k
        return ty // 2, ty % 2, tz // 2, tz % 2

    def distance(i, o):
        return far(i, roles) + far(o, n)

    distances = sorted({distance(i, o) for i, o in plane})

    def hop_two(e, i, o):
        part = xbuf.at[(x, *tile_place(e))]
        return remote(part, part, s2_s, s2_r.at[distances.index(distance(i, o))], in_plane(i, o))

    for e in range(per):
        if e == 0:

            @pl.when(self_one)
            def _():
                wait_bytes(a_recv.at[0, 0], s1_r.at[0])

            unless(self_one, lambda: wait_bytes(a_recv.at[0], s1_r.at[0]))
        else:
            wait_bytes(a_recv.at[e], s1_r.at[e])
        xbuf[(x, *tile_place(e))] = jnp.concatenate([a_recv[e, 0], a_recv[e, 1]], axis=0).astype(bf16)
        for i, o in plane:
            hop_two(e, i, o).start()

    def tiles(ref, core, role, at):
        if core == 0:
            return ref.at[role, :, at % 2, at // 2, at % 2]
        return ref.at[role, at // 2, at % 2, :, (at + 1) % 2]

    def hop_three(core, i, o):
        part = tiles(xbuf, core, (x + roles - i) % roles, (b + n - o) % n)
        return remote(part, part, d_s, d_r, (x, other))

    def cross_part(members):
        for core in range(2):

            @pl.when(k == core)
            def _(core=core):
                for i, o in members:
                    hop_three(core, i, o).start()

    cross_part([(0, 0)])
    for e, dist in enumerate(distances):
        pick_some(1 + e)
        members = [p for p in plane if distance(*p) == dist]
        wait_bytes(csend.at[:, pl.ds(0, len(members))], s2_r.at[e])
        cross_part(members)
    for e in range(1 + len(distances), len(cuts) - 1):
        pick_some(e)
    wait_bytes(drecv.at[:, :, 0], d_r)

    def part_of(i):
        return jnp.concatenate(
            [xbuf[r, i // 2, i % 2].reshape(m, L).astype(f32) for r in range(roles)], axis=1
        )

    def column_sums(blocks):
        total = functools.reduce(lambda u, v: u + v, [jnp.sum(v.reshape(m // 8, 8, width), axis=0) for v in blocks])
        return jnp.sum(total, axis=0, keepdims=True)

    mean = column_sums(part_of(i) for i in range(n)) / images
    centred = (part_of(i) - mean for i in range(n))
    inv_std = lax.rsqrt(column_sums(v * v for v in centred) / images + epsilon)

    first_lane = lax.broadcasted_iota(jnp.int32, (m, L), 1) == 0

    def forward(i):
        at = slice(i * m, (i + 1) * m)
        norm = (part_of(i) - mean) * inv_std
        inv = lax.rsqrt(jnp.sum(norm * norm, axis=1, keepdims=True) + epsilon)
        inorm[at, :] = jnp.broadcast_to(inv, (m, L))
        normed[at, :] = norm
        unit = (norm * inv).astype(bf16)
        feats[at, :] = unit
        cosine = jnp.dot(unit, wtrans[...], preferred_element_type=f32)
        label = labels[at, :]
        cos_pos = jnp.zeros((m, L), f32)
        sums = jnp.zeros((m, L), f32)
        for j in range(slots // L):
            lanes = slice(j * L, (j + 1) * L)
            hit = label == slot_ids[:, lanes]
            cos = cosine[:, lanes]
            term = jnp.where(hit, 0.0, jnp.exp(logit_scale * cos + slot_bias[:, lanes]))
            ebuf[at, lanes] = term
            sums += term
            cos_pos += jnp.where(hit, cos, 0.0)
        total = jnp.sum(cos_pos, axis=1, keepdims=True)
        pos_exp = jnp.broadcast_to(jnp.exp(margin_logit(total)), (m, L))
        posexp[at, :] = pos_exp
        sums += jnp.where(jnp.logical_and(first_lane, label >= 0.0), pos_exp, 0.0)
        part1[i : i + 1, :] = row_sum(sums)
        cosbuf[at, :] = cos_pos

    for i in range(n):
        forward(i)

    def sum_one(src, dst, sems, i, o):
        return remote(src, dst.at[x * n + b], sems.at[0], sems.at[1], in_plane(i, o))

    def sum_two(src, dst, sems, core, o):
        device = (x, c - k + core + ((a + o) % n - a) * step_a)
        return remote(src, dst.at[k * n + a], sems.at[0], sems.at[1], device)

    def each_two(src, dst, sems, act):
        for core in range(2):
            for o in sorted(range(1, n), key=lambda o: -far(o, n)):
                act(sum_two(src, dst, sems, core, o))
        act(remote(src, dst.at[k * n + a], sems.at[0], sems.at[1], (x, other)))

    def start_one(src, dst, sems):
        dst[x * n + b] = src[...]
        for i, o in plane:
            sum_one(src, dst, sems, i, o).start()

    def finish_one(src, dst, sems, total):
        wait_bytes(dst.at[pl.ds(0, peers)], sems.at[1])
        total[...] = add_all(dst, roles * n)

    def start_two(src, dst, sems):
        dst[k * n + a] = src[...]
        each_two(src, dst, sems, lambda copy: copy.start())

    def finish_two(src, dst, sems):
        wait_bytes(dst.at[pl.ds(0, 2 * n - 1)], sems.at[1])
        return add_all(dst, 2 * n)

    part_one = (part1, part1_in, p1)
    part_two = (part2, part2_in, p2)
    cos_one = (cos1, cos1_in, q1)
    cos_two = (cos2, cos2_in, q2)
    start_one(*part_one)
    for i in range(n):
        cos1[i : i + 1, :] = row_sum(cosbuf[i * m : (i + 1) * m, :])
    start_one(*cos_one)

    def by_terms(i, carry):
        at = pl.ds(pl.multiple_of(i * m, m), m)
        label = labels[at, :]
        hits = jnp.concatenate(
            [
                jnp.where(label == slot_ids[:, j * L : (j + 1) * L], 1.0, 0.0).astype(bf16)
                for j in range(slots // L)
            ],
            axis=1,
        )
        left = jnp.concatenate([ebuf[at, :].astype(bf16), hits], axis=0)
        both = jnp.dot(left, wround[...], preferred_element_type=f32)
        inv = wide(inorm[at, :], width)
        unit = normed[at, :] * inv
        for out, term in ((qn, both[:m]), (qw, both[m:])):
            radial = jnp.sum(unit * term, axis=1, keepdims=True)
            out[at, :] = (term - unit * radial) * inv
        return carry

    lax.fori_loop(0, n * 5 // 8, by_terms, 0)

    finish_one(*part_one, part2)
    start_two(*part_two)

    lax.fori_loop(n * 5 // 8, n, by_terms, 0)

    total = finish_two(*part_two)
    log_sum = jnp.log(total)
    scale[...] = logit_scale / total

    def factors(i, at):
        plain = column(scale[pl.ds(i, 1), :])
        return plain, (posexp[at, :] * plain - logit_scale).astype(bf16).astype(f32)

    values = []
    for i in range(n):
        at = slice(i * m, (i + 1) * m)
        plain, hit = factors(i, at)
        value = qn[at, :] * wide(plain, width) + qw[at, :] * wide(hit, width)
        qn[at, :] = value
        fold = [jnp.sum(v.reshape(m // 8, 8, width), axis=0) for v in (value, value * normed[at, :])]
        values = [u + v for u, v in zip(values, fold)] if values else fold
    shift, slope = (jnp.sum(v, axis=0, keepdims=True) / images for v in values)

    def finish(core, out):
        def block(i, carry):
            p = (i + core) % 2
            for j in range(per):
                at = pl.ds(pl.multiple_of(i * m + (2 * j + p) * rows, rows), rows)
                value = (qn[at, :] - shift - normed[at, :] * slope) * inv_std
                for r in range(roles):
                    out[r, i // 2, i % 2, j, p] = value[:, r * L : (r + 1) * L].astype(out.dtype)
            return carry

        lax.fori_loop(0, n, block, 0, unroll=4 if n % 4 == 0 else 1)

    finish(1 - k, fsend)

    by_far = sorted(range(n), key=lambda o: -far(o, n))

    def cross(core, i):
        every = pl.ds(0, roles)
        return remote(
            tiles(fsend, 1 - core, every, i), tiles(drecv, 1 - core, every, i), ds_s, ds_r.at[i], (x, other)
        )

    for core in range(2):

        @pl.when(k == core)
        def _(core=core):
            for o in by_far:
                cross(core, (a + o) % n).start()

    finish(k, qbuf)

    def tile_of(at, e):
        return ((a + jnp.where((a + at + k) % 2 == 0, near[0][e], near[1][e])) % n) // 2

    def reduce_two(e, f, i, o):
        return remote(csend.at[e, f], crecv.at[e, f], r2_s, r2_r.at[e], in_plane(i, o))

    arrived = set()

    def cross_wait(o):
        if o not in arrived:
            arrived.add(o)
            wait_bytes(tiles(drecv, 0, pl.ds(0, roles), 0), ds_r.at[(b + o) % n])

    def both(e, role, at):
        i = tile_of(at, e)
        ay, by = i, at // 2
        pa, pb = (at + k) % 2, at % 2
        place = (role, ay + (by - ay) * k, pa + (pb - pa) * k, by + (ay - by) * k, pb + (pa - pb) * k)
        return qbuf[place] + drecv[place].astype(f32)

    for e in reversed(range(per)):
        for f, (i, o) in enumerate(plane):
            cross_wait(o)
            csend[e, f] = both(e, (x + i) % roles, (b + o) % n).astype(bf16)
            reduce_two(e, f, i, o).start()
        cross_wait(0)
        csum[e] = both(e, x, b)

    finish_one(*cos_one, cos2)
    start_two(*cos_two)

    def logit_grad(i, carry):
        at = pl.ds(pl.multiple_of(i * m, m), m)
        plain, hit = factors(i, at)
        label = labels[at, :]
        for j in range(slots // L):
            lanes = slice(j * L, (j + 1) * L)
            gbuf[at, lanes] = jnp.where(label == slot_ids[:, lanes], hit, ebuf[at, lanes] * plain).astype(bf16)
        return carry

    lax.fori_loop(0, n, logit_grad, 0)

    def by_centre(i, carry):
        at = pl.ds(pl.multiple_of(i * L, L), L)
        back = lax.dot_general(gbuf[:, at], feats[...], (((0,), (0,)), ((), ())), preferred_element_type=f32)
        inv = wide(winv[at, :], width)
        unit = picked[at, :].astype(f32) * inv
        radial = jnp.sum(unit * back, axis=1, keepdims=True)
        cgbuf[at, :] = ((back - unit * radial) * inv).astype(bf16)
        return carry

    lax.fori_loop(0, slots // L, by_centre, 0)

    losses = log_sum - margin_logit(finish_two(*cos_two))
    row = lax.broadcasted_iota(jnp.int32, (n, L), 0)
    losses = jnp.sum(jnp.where(row == y, losses, 0.0), axis=0, keepdims=True)
    losses = pltpu.roll(jnp.broadcast_to(losses, (8, L)), (L - z * rows - k * own) % L, 1)
    loss[...] = losses[0:1, :own]

    def reduce_one(e, core):
        device = (x, c - k + core + ((a + jnp.where(self_one, near[0][e], near[1][e])) % n - a) * step_a)
        return remote(asrc.at[e, core], arecv.at[a], r1.at[0], r1.at[1], device)

    for e in reversed(range(per)):
        wait_bytes(crecv.at[e], r2_r.at[e])
        terms = [csum[e]] + [crecv[e, f].astype(f32) for f in range(peers)]
        while len(terms) > 1:
            terms = [terms[i] + terms[i + 1] for i in range(0, len(terms), 2)]
        for core in range(2):
            asrc[e, core] = terms[0][core * own : (core + 1) * own, :]
        if e:
            for core in range(2):
                reduce_one(e, core).start()
        else:
            for core in range(2):
                me = jnp.logical_and(self_one, k == core)
                unless(me, lambda core: reduce_one(0, core).start(), core)

                @pl.when(me)
                def _(core=core):
                    arecv[a] = asrc[0, core]

    @pl.when(self_one)
    def _():
        wait_bytes(arecv.at[pl.ds(0, n - 1)], r1.at[1])

    unless(self_one, lambda: wait_bytes(arecv, r1.at[1]))
    fg[...] = add_all(arecv, n)

    @pl.when(self_one)
    def _():
        wait_bytes(arecv.at[pl.ds(0, n - 1)], s1_s)
        wait_bytes(arecv.at[pl.ds(0, n - 1)], r1.at[0])

    @pl.when(jnp.logical_not(self_one))
    def _():
        wait_bytes(arecv, s1_s)
        wait_bytes(arecv, r1.at[0])

    wait_bytes(csend, s2_s)
    wait_bytes(drecv.at[:, :, 0], d_s)
    wait_bytes(drecv.at[:, :, 0], ds_s)
    wait_bytes(csend, r2_s)
    for sems in (p1, q1):
        wait_bytes(part1_in.at[pl.ds(0, peers)], sems.at[0])
    for sems in (p2, q2):
        wait_bytes(part2_in.at[pl.ds(0, 2 * n - 1)], sems.at[0])


def hand_on(fg_in, cg_in, loss_in, fg_out, cg_out, loss_out, sem):
    parts = 8
    size = cg_in.shape[0] // parts
    pairs = [(fg_in, fg_out), (loss_in, loss_out)]
    pairs += [tuple(ref.at[pl.ds(i * size, size)] for ref in (cg_in, cg_out)) for i in range(parts)]
    copies = [pltpu.make_async_copy(src, dst, sem.at[i]) for i, (src, dst) in enumerate(pairs)]
    for copy in copies:
        copy.start()
    for copy in copies:
        copy.wait()


def body(n, roles, features, centres, samples, counts, label_row, owner):
    own = features.shape[0]
    rows = 2 * own
    images = label_row.shape[0]
    slots = samples.shape[1]
    held, width = centres.shape
    per = n // 2
    peers = roles * n - 1
    distances = roles // 2 + n // 2
    tiles = (roles, per, 2, per, 2, rows, L)
    dma = pltpu.SemaphoreType.DMA
    anywhere = pl.BlockSpec(memory_space=pl.ANY)
    vmem = pl.BlockSpec(memory_space=pltpu.VMEM)
    hbm = pl.BlockSpec(memory_space=pltpu.HBM)
    out_shape = (
        jax.ShapeDtypeStruct(features.shape, f32),
        jax.ShapeDtypeStruct((slots, width), bf16),
        jax.ShapeDtypeStruct((1, own), f32),
    )
    results = pl.pallas_call(
        functools.partial(kernel, n, roles, rows, slots, held),
        out_shape=tuple(pltpu.VMEM(s.shape, s.dtype) for s in out_shape),
        in_specs=[hbm] * 6,
        out_specs=(vmem,) * 3,
        scratch_shapes=[
            pltpu.VMEM(features.shape, bf16),
            pltpu.VMEM((1, slots), jnp.int32),
            pltpu.VMEM((2, 1, images), jnp.int32),
            pltpu.SMEM((1, 1), jnp.int32),
            pltpu.VMEM((held, width), bf16),
            pltpu.VMEM((slots, width), bf16),
            pltpu.VMEM((slots, width), bf16),
            pltpu.VMEM((width, slots), bf16),
            pltpu.VMEM((slots, L), f32),
            pltpu.VMEM((images, L), f32),
            pltpu.VMEM(tiles, bf16),
            pltpu.VMEM((images, width), bf16),
            pltpu.VMEM((images, width), f32),
            pltpu.VMEM((images, L), f32),
            pltpu.VMEM((images, slots), f32),
            pltpu.VMEM((images, L), f32),
            pltpu.VMEM((images, width), f32),
            pltpu.VMEM((images, width), f32),
            pltpu.VMEM((images, slots), bf16),
            pltpu.VMEM(tiles, f32),
            pltpu.VMEM((own, L), f32),
            pltpu.VMEM((per, 2, own, L), f32),
            pltpu.VMEM((n, L), f32),
            pltpu.VMEM((n, L), f32),
            pltpu.VMEM((n, L), f32),
            pltpu.VMEM((n, L), f32),
            pltpu.VMEM((images, L), f32),
            pltpu.VMEM((n, L), f32),
            pltpu.VMEM((roles * n, n, L), f32),
            pltpu.VMEM((2 * n, n, L), f32),
            pltpu.VMEM((roles * n, n, L), f32),
            pltpu.VMEM((2 * n, n, L), f32),
            pltpu.VMEM(tiles, bf16),
            pltpu.VMEM(tiles, bf16),
            pltpu.VMEM((per, peers, rows, L), bf16),
            pltpu.VMEM((per, rows, L), f32),
            pltpu.VMEM((per, peers, rows, L), bf16),
            pltpu.VMEM((per, 2, own, L), f32),
            pltpu.VMEM((n, own, L), f32),
            dma((6,)),
            dma(()), dma((per,)),
            dma(()), dma((distances,)),
            dma(()), dma(()),
            dma((2,)), dma((2,)), dma((2,)), dma((2,)),
            dma(()), dma((n,)),
            dma(()), dma((per,)),
            dma((2,)),
        ],
        compiler_params=pltpu.CompilerParams(
            collective_id=0, has_side_effects=True, vmem_limit_bytes=56 * 1024 * 1024
        ),
    )(features, centres, samples, counts[None], label_row[None], owner[None])
    feature_grad, centre_grad, loss = pl.pallas_call(
        hand_on,
        out_shape=out_shape,
        in_specs=[vmem] * 3,
        out_specs=(anywhere,) * 3,
        scratch_shapes=[dma((10,))],
    )(*(pltpu.with_memory_space_constraint(r, pltpu.VMEM) for r in results))
    return feature_grad, centre_grad[None], loss[0]


def solution(mesh):
    n = math.isqrt(mesh.shape["cls"] // 2)
    return jax.shard_map(
        functools.partial(body, n, mesh.shape["role"]),
        mesh=mesh,
        in_specs=(
            P("cls", "role"),
            P(("role", "cls"), None),
            P(("role", "cls"), None),
            P(("role", "cls")),
            P(),
            P(),
        ),
        out_specs=(P("cls", "role"), P(("role", "cls"), None, None), P("cls")),
        check_vma=False,
    )
```

```python
import functools
import math

import jax
import jax.numpy as jnp
from jax import lax
from jax.experimental import pallas as pl
from jax.experimental.pallas import tpu as pltpu
from jax.sharding import PartitionSpec as P

logit_scale = 64.0
margin_cos = math.cos(0.5)
margin_sin = math.sin(0.5)
epsilon = 1e-05

MESH = pl.DeviceIdType.MESH
f32 = jnp.float32
bf16 = jnp.bfloat16
L = 128


def column(row):
    return jnp.transpose(jnp.broadcast_to(row, (L, L)))


def row_sum(block):
    return jnp.sum(jnp.transpose(block), axis=0, keepdims=True)


def margin_logit(cos):
    sine = jnp.sqrt(jnp.maximum(1.0 - cos * cos, 0.0))
    return logit_scale * (cos * margin_cos - sine * margin_sin)


def wide(block, width):
    return jnp.concatenate([block] * (width // L), axis=1)


def add_all(ref, count):
    terms = [ref[i] for i in range(count)]
    while len(terms) > 1:
        terms = [terms[i] + terms[i + 1] for i in range(0, len(terms), 2)]
    return terms[0]


def kernel(
    n, roles, rows, slots, held,
    feat_hbm, cen_hbm, samp_hbm, count_hbm, label_hbm, owner_hbm,
    fg, cgbuf, loss,
    feat, samp_row, ints, count, cen, picked, wround, wtrans, winv, labels, xbuf, feats, normed, inorm,
    ebuf, posexp, qn, qw, gbuf, qbuf, a_src, a_recv, part1, part2, cos1, cos2, cosbuf, scale,
    part1_in, part2_in, cos1_in, cos2_in, fsend, drecv, csend, csum, crecv, asrc, arecv,
    in_sem, s1_s, s1_r, s2_s, s2_r, d_s, d_r, p1, p2, q1, q2, ds_s, ds_r, r2_s, r2_r, r1,
):
    x = lax.axis_index("role")
    c = lax.axis_index("cls")
    k = c % 2
    t = c // 2
    y = t // n
    z = t % n
    width = L * roles
    own = rows // 2
    per = n // 2
    images = n * n * rows
    m = n * rows
    a = y + (z - y) * k
    b = z + (y - z) * k
    step_a = 2 * n - (2 * n - 2) * k
    step_b = 2 + (2 * n - 2) * k
    other = c + 1 - 2 * k
    q = (y + z) % 2
    aq = y + (z - y) * q
    step_q = 2 * n - (2 * n - 2) * q
    parity = (b + k) % 2
    self_one = k == q

    def remote(src, dst, send, recv, device):
        return pltpu.make_async_remote_copy(
            src_ref=src, dst_ref=dst, send_sem=send, recv_sem=recv, device_id=device, device_id_type=MESH
        )

    def wait_bytes(ref, sem):
        pltpu.make_async_copy(ref, ref, sem).wait()

    def far(o, size):
        return min(o, size - o)

    plane = [(i, o) for i in range(roles) for o in range(n)][1:]
    plane = sorted(plane, key=lambda p: -(far(p[0], roles) + far(p[1], n)))
    peers = len(plane)
    near = [sorted(range(p, n, 2), key=lambda o: far(o, n)) for p in range(2)]

    def in_plane(i, o):
        return (x + i) % roles, c + ((b + o) % n - b) * step_b

    feat_copy = pltpu.make_async_copy(feat_hbm, feat, in_sem.at[0])
    centre_copy = pltpu.make_async_copy(cen_hbm, cen, in_sem.at[1])
    count_copy = pltpu.make_async_copy(count_hbm, count, in_sem.at[2])
    int_copies = [
        pltpu.make_async_copy(src, dst, in_sem.at[3 + i])
        for i, (src, dst) in enumerate(((samp_hbm, samp_row), (label_hbm, ints.at[0]), (owner_hbm, ints.at[1])))
    ]
    for copy in (feat_copy, *int_copies, count_copy, centre_copy):
        copy.start()

    barrier = pltpu.get_barrier_semaphore()

    def signal(device):
        pl.semaphore_signal(barrier, inc=1, device_id=device, device_id_type=MESH)

    def unless(condition, fn, *args):
        pl.when(jnp.logical_not(condition))(functools.partial(fn, *args))

    for i, o in plane:
        signal(in_plane(i, o))
    for core in range(2):
        at, step = (y, 2 * n) if core == 0 else (z, 2)
        for o in range(1, n):
            signal((x, c - k + core + ((at + o) % n - at) * step))
    signal((x, other))
    target_one = [(x, c - k + q + ((aq + o) % n - aq) * step_q) for o in range(n)]
    source_one = {
        (i, core): (x, c - k + core + (2 * i + parity - a) * step_a) for i in range(per) for core in range(2)
    }

    def is_me(i, core):
        return jnp.logical_and(2 * i + parity == a, k == core)

    for o in range(1, n):
        signal(target_one[o])
    unless(self_one, signal, target_one[0])
    for key in source_one:
        unless(is_me(*key), signal, source_one[key])

    feat_copy.wait()
    a_src[...] = feat[...].astype(f32)
    pl.semaphore_wait(barrier, peers + 4 * n - 1 - 2 * self_one.astype(jnp.int32))

    def hop_one(o):
        e = near[o % 2].index((n - o) % n)
        return remote(a_src, a_recv.at[e, k], s1_s, s1_r.at[e], target_one[o])

    for o in sorted(range(1, n), key=lambda o: -far(o, n)):
        hop_one(o).start()
    unless(self_one, lambda: hop_one(0).start())

    @pl.when(self_one)
    def _():
        a_recv[0, k] = a_src[...]

    for copy in int_copies:
        copy.wait()
    count_copy.wait()
    shard = x * (2 * n * n) + c
    label_eff = jnp.where(ints[1] == shard, ints[0], -1).astype(f32)
    for i in range(images // L):
        labels[i * L : (i + 1) * L, :] = column(label_eff[:, i * L : (i + 1) * L])
    slot = lax.broadcasted_iota(jnp.int32, (1, slots), 1)
    usable = slot < count[0, 0]
    slot_ids = jnp.where(usable, samp_row[...], -2).astype(f32)
    slot_bias = jnp.where(usable, 0.0, -1e30).astype(f32)
    centre_copy.wait()

    lane = lax.broadcasted_iota(jnp.int32, (L, L), 1).astype(f32)

    def pick(i, carry):
        at = pl.ds(pl.multiple_of(i * L, L), L)
        ids = column(samp_row[:, at].astype(f32))
        hot = [jnp.where(ids == lane + (j * L), 1.0, 0.0).astype(bf16) for j in range(held // L)]
        rows_f = jnp.dot(jnp.concatenate(hot, axis=1), cen[...], preferred_element_type=f32)
        picked[at, :] = rows_f.astype(bf16)
        inv = lax.rsqrt(jnp.sum(rows_f * rows_f, axis=1, keepdims=True) + epsilon)
        unit = rows_f * inv
        winv[at, :] = jnp.broadcast_to(inv, (L, L))
        wround[at, :] = unit.astype(bf16)
        wtrans[:, at] = jnp.transpose(unit).astype(bf16)
        return carry

    blocks = slots // L
    cuts = [blocks * i // 8 for i in (0, 1, 3, 4, 5, 6, 7, 8)]

    def pick_some(i):
        if cuts[i] < cuts[i + 1]:
            lax.fori_loop(cuts[i], cuts[i + 1], pick, 0)

    pick_some(0)

    def tile_place(e):
        at = (a + jnp.where(self_one, near[0][e], near[1][e])) % n
        ty, tz = at + (y - at) * k, z + (at - z) * k
        return ty // 2, ty % 2, tz // 2, tz % 2

    def distance(i, o):
        return far(i, roles) + far(o, n)

    distances = sorted({distance(i, o) for i, o in plane})

    def hop_two(e, i, o):
        part = xbuf.at[(x, *tile_place(e))]
        return remote(part, part, s2_s, s2_r.at[distances.index(distance(i, o))], in_plane(i, o))

    for e in range(per):
        if e == 0:

            @pl.when(self_one)
            def _():
                wait_bytes(a_recv.at[0, 0], s1_r.at[0])

            unless(self_one, lambda: wait_bytes(a_recv.at[0], s1_r.at[0]))
        else:
            wait_bytes(a_recv.at[e], s1_r.at[e])
        xbuf[(x, *tile_place(e))] = jnp.concatenate([a_recv[e, 0], a_recv[e, 1]], axis=0).astype(bf16)
        for i, o in plane:
            hop_two(e, i, o).start()

    def tiles(ref, core, role, at):
        if core == 0:
            return ref.at[role, :, at % 2, at // 2, at % 2]
        return ref.at[role, at // 2, at % 2, :, (at + 1) % 2]

    def hop_three(core, i, o):
        part = tiles(xbuf, core, (x + roles - i) % roles, (b + n - o) % n)
        return remote(part, part, d_s, d_r, (x, other))

    def cross_part(members):
        for core in range(2):

            @pl.when(k == core)
            def _(core=core):
                for i, o in members:
                    hop_three(core, i, o).start()

    cross_part([(0, 0)])
    for e, dist in enumerate(distances):
        pick_some(1 + e)
        members = [p for p in plane if distance(*p) == dist]
        wait_bytes(csend.at[:, pl.ds(0, len(members))], s2_r.at[e])
        cross_part(members)
    for e in range(1 + len(distances), len(cuts) - 1):
        pick_some(e)
    wait_bytes(drecv.at[:, :, 0], d_r)

    def part_of(i):
        return jnp.concatenate(
            [xbuf[r, i // 2, i % 2].reshape(m, L).astype(f32) for r in range(roles)], axis=1
        )

    def column_sums(blocks):
        total = functools.reduce(lambda u, v: u + v, [jnp.sum(v.reshape(m // 8, 8, width), axis=0) for v in blocks])
        return jnp.sum(total, axis=0, keepdims=True)

    mean = column_sums(part_of(i) for i in range(n)) / images
    centred = (part_of(i) - mean for i in range(n))
    inv_std = lax.rsqrt(column_sums(v * v for v in centred) / images + epsilon)

    first_lane = lax.broadcasted_iota(jnp.int32, (m, L), 1) == 0

    def forward(i):
        at = slice(i * m, (i + 1) * m)
        norm = (part_of(i) - mean) * inv_std
        inv = lax.rsqrt(jnp.sum(norm * norm, axis=1, keepdims=True) + epsilon)
        inorm[at, :] = jnp.broadcast_to(inv, (m, L))
        normed[at, :] = norm
        unit = (norm * inv).astype(bf16)
        feats[at, :] = unit
        cosine = jnp.dot(unit, wtrans[...], preferred_element_type=f32)
        label = labels[at, :]
        cos_pos = jnp.zeros((m, L), f32)
        sums = jnp.zeros((m, L), f32)
        for j in range(slots // L):
            lanes = slice(j * L, (j + 1) * L)
            hit = label == slot_ids[:, lanes]
            cos = cosine[:, lanes]
            term = jnp.where(hit, 0.0, jnp.exp(logit_scale * cos + slot_bias[:, lanes]))
            ebuf[at, lanes] = term
            sums += term
            cos_pos += jnp.where(hit, cos, 0.0)
        total = jnp.sum(cos_pos, axis=1, keepdims=True)
        pos_exp = jnp.broadcast_to(jnp.exp(margin_logit(total)), (m, L))
        posexp[at, :] = pos_exp
        sums += jnp.where(jnp.logical_and(first_lane, label >= 0.0), pos_exp, 0.0)
        part1[i : i + 1, :] = row_sum(sums)
        cosbuf[at, :] = cos_pos

    for i in range(n):
        forward(i)

    def sum_one(src, dst, sems, i, o):
        return remote(src, dst.at[x * n + b], sems.at[0], sems.at[1], in_plane(i, o))

    def sum_two(src, dst, sems, core, o):
        device = (x, c - k + core + ((a + o) % n - a) * step_a)
        return remote(src, dst.at[k * n + a], sems.at[0], sems.at[1], device)

    def each_two(src, dst, sems, act):
        for core in range(2):
            for o in sorted(range(1, n), key=lambda o: -far(o, n)):
                act(sum_two(src, dst, sems, core, o))
        act(remote(src, dst.at[k * n + a], sems.at[0], sems.at[1], (x, other)))

    def start_one(src, dst, sems):
        dst[x * n + b] = src[...]
        for i, o in plane:
            sum_one(src, dst, sems, i, o).start()

    def finish_one(src, dst, sems, total):
        wait_bytes(dst.at[pl.ds(0, peers)], sems.at[1])
        total[...] = add_all(dst, roles * n)

    def start_two(src, dst, sems):
        dst[k * n + a] = src[...]
        each_two(src, dst, sems, lambda copy: copy.start())

    def finish_two(src, dst, sems):
        wait_bytes(dst.at[pl.ds(0, 2 * n - 1)], sems.at[1])
        return add_all(dst, 2 * n)

    part_one = (part1, part1_in, p1)
    part_two = (part2, part2_in, p2)
    cos_one = (cos1, cos1_in, q1)
    cos_two = (cos2, cos2_in, q2)
    start_one(*part_one)
    for i in range(n):
        cos1[i : i + 1, :] = row_sum(cosbuf[i * m : (i + 1) * m, :])
    start_one(*cos_one)

    def by_terms(i, carry):
        at = pl.ds(pl.multiple_of(i * m, m), m)
        label = labels[at, :]
        hits = jnp.concatenate(
            [
                jnp.where(label == slot_ids[:, j * L : (j + 1) * L], 1.0, 0.0).astype(bf16)
                for j in range(slots // L)
            ],
            axis=1,
        )
        left = jnp.concatenate([ebuf[at, :].astype(bf16), hits], axis=0)
        both = jnp.dot(left, wround[...], preferred_element_type=f32)
        inv = wide(inorm[at, :], width)
        unit = normed[at, :] * inv
        for out, term in ((qn, both[:m]), (qw, both[m:])):
            radial = jnp.sum(unit * term, axis=1, keepdims=True)
            out[at, :] = (term - unit * radial) * inv
        return carry

    lax.fori_loop(0, n * 5 // 8, by_terms, 0)

    finish_one(*part_one, part2)
    start_two(*part_two)

    lax.fori_loop(n * 5 // 8, n, by_terms, 0)

    total = finish_two(*part_two)
    log_sum = jnp.log(total)
    scale[...] = logit_scale / total

    def factors(i, at):
        plain = column(scale[pl.ds(i, 1), :])
        return plain, (posexp[at, :] * plain - logit_scale).astype(bf16).astype(f32)

    values = []
    for i in range(n):
        at = slice(i * m, (i + 1) * m)
        plain, hit = factors(i, at)
        value = qn[at, :] * wide(plain, width) + qw[at, :] * wide(hit, width)
        qn[at, :] = value
        fold = [jnp.sum(v.reshape(m // 8, 8, width), axis=0) for v in (value, value * normed[at, :])]
        values = [u + v for u, v in zip(values, fold)] if values else fold
    shift, slope = (jnp.sum(v, axis=0, keepdims=True) / images for v in values)

    def finish(core, out):
        def block(i, carry):
            p = (i + core) % 2
            for j in range(per):
                at = pl.ds(pl.multiple_of(i * m + (2 * j + p) * rows, rows), rows)
                value = (qn[at, :] - shift - normed[at, :] * slope) * inv_std
                for r in range(roles):
                    out[r, i // 2, i % 2, j, p] = value[:, r * L : (r + 1) * L].astype(out.dtype)
            return carry

        lax.fori_loop(0, n, block, 0, unroll=4 if n % 4 == 0 else 1)

    finish(1 - k, fsend)

    by_far = sorted(range(n), key=lambda o: -far(o, n))

    def cross(core, i):
        every = pl.ds(0, roles)
        return remote(
            tiles(fsend, 1 - core, every, i), tiles(drecv, 1 - core, every, i), ds_s, ds_r.at[i], (x, other)
        )

    for core in range(2):

        @pl.when(k == core)
        def _(core=core):
            for o in by_far:
                cross(core, (a + o) % n).start()

    finish(k, qbuf)

    def tile_of(at, e):
        return ((a + jnp.where((a + at + k) % 2 == 0, near[0][e], near[1][e])) % n) // 2

    def reduce_two(e, f, i, o):
        return remote(csend.at[e, f], crecv.at[e, f], r2_s, r2_r.at[e], in_plane(i, o))

    arrived = set()

    def cross_wait(o):
        if o not in arrived:
            arrived.add(o)
            wait_bytes(tiles(drecv, 0, pl.ds(0, roles), 0), ds_r.at[(b + o) % n])

    def both(e, role, at):
        i = tile_of(at, e)
        ay, by = i, at // 2
        pa, pb = (at + k) % 2, at % 2
        place = (role, ay + (by - ay) * k, pa + (pb - pa) * k, by + (ay - by) * k, pb + (pa - pb) * k)
        return qbuf[place] + drecv[place].astype(f32)

    for e in reversed(range(per)):
        for f, (i, o) in enumerate(plane):
            cross_wait(o)
            csend[e, f] = both(e, (x + i) % roles, (b + o) % n).astype(bf16)
            reduce_two(e, f, i, o).start()
        cross_wait(0)
        csum[e] = both(e, x, b)

    finish_one(*cos_one, cos2)
    start_two(*cos_two)

    def logit_grad(i, carry):
        at = pl.ds(pl.multiple_of(i * m, m), m)
        plain, hit = factors(i, at)
        label = labels[at, :]
        for j in range(slots // L):
            lanes = slice(j * L, (j + 1) * L)
            gbuf[at, lanes] = jnp.where(label == slot_ids[:, lanes], hit, ebuf[at, lanes] * plain).astype(bf16)
        return carry

    lax.fori_loop(0, n, logit_grad, 0)

    def by_centre(i, carry):
        at = pl.ds(pl.multiple_of(i * L, L), L)
        back = lax.dot_general(gbuf[:, at], feats[...], (((0,), (0,)), ((), ())), preferred_element_type=f32)
        inv = wide(winv[at, :], width)
        unit = picked[at, :].astype(f32) * inv
        radial = jnp.sum(unit * back, axis=1, keepdims=True)
        cgbuf[at, :] = ((back - unit * radial) * inv).astype(bf16)
        return carry

    lax.fori_loop(0, slots // L, by_centre, 0)

    losses = log_sum - margin_logit(finish_two(*cos_two))
    row = lax.broadcasted_iota(jnp.int32, (n, L), 0)
    losses = jnp.sum(jnp.where(row == y, losses, 0.0), axis=0, keepdims=True)
    losses = pltpu.roll(jnp.broadcast_to(losses, (8, L)), (L - z * rows - k * own) % L, 1)
    loss[...] = losses[0:1, :own]

    def reduce_one(e, core):
        device = (x, c - k + core + ((a + jnp.where(self_one, near[0][e], near[1][e])) % n - a) * step_a)
        return remote(asrc.at[e, core], arecv.at[a], r1.at[0], r1.at[1], device)

    for e in reversed(range(per)):
        wait_bytes(crecv.at[e], r2_r.at[e])
        terms = [csum[e]] + [crecv[e, f].astype(f32) for f in range(peers)]
        while len(terms) > 1:
            terms = [terms[i] + terms[i + 1] for i in range(0, len(terms), 2)]
        for core in range(2):
            asrc[e, core] = terms[0][core * own : (core + 1) * own, :]
        if e:
            for core in range(2):
                reduce_one(e, core).start()
        else:
            for core in range(2):
                me = jnp.logical_and(self_one, k == core)
                unless(me, lambda core: reduce_one(0, core).start(), core)

                @pl.when(me)
                def _(core=core):
                    arecv[a] = asrc[0, core]

    @pl.when(self_one)
    def _():
        wait_bytes(arecv.at[pl.ds(0, n - 1)], r1.at[1])

    unless(self_one, lambda: wait_bytes(arecv, r1.at[1]))
    fg[...] = add_all(arecv, n)

    @pl.when(self_one)
    def _():
        wait_bytes(arecv.at[pl.ds(0, n - 1)], s1_s)
        wait_bytes(arecv.at[pl.ds(0, n - 1)], r1.at[0])

    @pl.when(jnp.logical_not(self_one))
    def _():
        wait_bytes(arecv, s1_s)
        wait_bytes(arecv, r1.at[0])

    wait_bytes(csend, s2_s)
    wait_bytes(drecv.at[:, :, 0], d_s)
    wait_bytes(drecv.at[:, :, 0], ds_s)
    wait_bytes(csend, r2_s)
    for sems in (p1, q1):
        wait_bytes(part1_in.at[pl.ds(0, peers)], sems.at[0])
    for sems in (p2, q2):
        wait_bytes(part2_in.at[pl.ds(0, 2 * n - 1)], sems.at[0])


def hand_on(fg_in, cg_in, loss_in, fg_out, cg_out, loss_out, sem):
    parts = 8
    size = cg_in.shape[0] // parts
    pairs = [(fg_in, fg_out), (loss_in, loss_out)]
    pairs += [tuple(ref.at[pl.ds(i * size, size)] for ref in (cg_in, cg_out)) for i in range(parts)]
    copies = [pltpu.make_async_copy(src, dst, sem.at[i]) for i, (src, dst) in enumerate(pairs)]
    for copy in copies:
        copy.start()
    for copy in copies:
        copy.wait()


def body(n, roles, features, centres, samples, counts, label_row, owner):
    own = features.shape[0]
    rows = 2 * own
    images = label_row.shape[0]
    slots = samples.shape[1]
    held, width = centres.shape
    per = n // 2
    peers = roles * n - 1
    distances = roles // 2 + n // 2
    tiles = (roles, per, 2, per, 2, rows, L)
    dma = pltpu.SemaphoreType.DMA
    anywhere = pl.BlockSpec(memory_space=pl.ANY)
    vmem = pl.BlockSpec(memory_space=pltpu.VMEM)
    hbm = pl.BlockSpec(memory_space=pltpu.HBM)
    out_shape = (
        jax.ShapeDtypeStruct(features.shape, f32),
        jax.ShapeDtypeStruct((slots, width), bf16),
        jax.ShapeDtypeStruct((1, own), f32),
    )
    results = pl.pallas_call(
        functools.partial(kernel, n, roles, rows, slots, held),
        out_shape=tuple(pltpu.VMEM(s.shape, s.dtype) for s in out_shape),
        in_specs=[hbm] * 6,
        out_specs=(vmem,) * 3,
        scratch_shapes=[
            pltpu.VMEM(features.shape, bf16),
            pltpu.VMEM((1, slots), jnp.int32),
            pltpu.VMEM((2, 1, images), jnp.int32),
            pltpu.SMEM((1, 1), jnp.int32),
            pltpu.VMEM((held, width), bf16),
            pltpu.VMEM((slots, width), bf16),
            pltpu.VMEM((slots, width), bf16),
            pltpu.VMEM((width, slots), bf16),
            pltpu.VMEM((slots, L), f32),
            pltpu.VMEM((images, L), f32),
            pltpu.VMEM(tiles, bf16),
            pltpu.VMEM((images, width), bf16),
            pltpu.VMEM((images, width), f32),
            pltpu.VMEM((images, L), f32),
            pltpu.VMEM((images, slots), f32),
            pltpu.VMEM((images, L), f32),
            pltpu.VMEM((images, width), f32),
            pltpu.VMEM((images, width), f32),
            pltpu.VMEM((images, slots), bf16),
            pltpu.VMEM(tiles, f32),
            pltpu.VMEM((own, L), f32),
            pltpu.VMEM((per, 2, own, L), f32),
            pltpu.VMEM((n, L), f32),
            pltpu.VMEM((n, L), f32),
            pltpu.VMEM((n, L), f32),
            pltpu.VMEM((n, L), f32),
            pltpu.VMEM((images, L), f32),
            pltpu.VMEM((n, L), f32),
            pltpu.VMEM((roles * n, n, L), f32),
            pltpu.VMEM((2 * n, n, L), f32),
            pltpu.VMEM((roles * n, n, L), f32),
            pltpu.VMEM((2 * n, n, L), f32),
            pltpu.VMEM(tiles, bf16),
            pltpu.VMEM(tiles, bf16),
            pltpu.VMEM((per, peers, rows, L), bf16),
            pltpu.VMEM((per, rows, L), f32),
            pltpu.VMEM((per, peers, rows, L), bf16),
            pltpu.VMEM((per, 2, own, L), f32),
            pltpu.VMEM((n, own, L), f32),
            dma((6,)),
            dma(()), dma((per,)),
            dma(()), dma((distances,)),
            dma(()), dma(()),
            dma((2,)), dma((2,)), dma((2,)), dma((2,)),
            dma(()), dma((n,)),
            dma(()), dma((per,)),
            dma((2,)),
        ],
        compiler_params=pltpu.CompilerParams(
            collective_id=0, has_side_effects=True, vmem_limit_bytes=56 * 1024 * 1024
        ),
    )(features, centres, samples, counts[None], label_row[None], owner[None])
    feature_grad, centre_grad, loss = pl.pallas_call(
        hand_on,
        out_shape=out_shape,
        in_specs=[vmem] * 3,
        out_specs=(anywhere,) * 3,
        scratch_shapes=[dma((10,))],
    )(*(pltpu.with_memory_space_constraint(r, pltpu.VMEM) for r in results))
    return feature_grad, centre_grad[None], loss[0]


def solution(mesh):
    n = math.isqrt(mesh.shape["cls"] // 2)
    return jax.shard_map(
        functools.partial(body, n, mesh.shape["role"]),
        mesh=mesh,
        in_specs=(
            P("cls", "role"),
            P(("role", "cls"), None),
            P(("role", "cls"), None),
            P(("role", "cls")),
            P(),
            P(),
        ),
        out_specs=(P("cls", "role"), P(("role", "cls"), None, None), P("cls")),
        check_vma=False,
    )
```
